128 devices in a mesh: dom: 16 (over x_hi, y, core), vol: 8 (over z, x_lo).
Axes of the slice: x: 4 (x_hi: 2, x_lo: 2; x = x_hi * 2 + x_lo), y: 4, z: 4, core: 2. Of those that a mesh axis runs over, the one named last changes fastest.
Arguments:
- volume: bfloat16 [4, 256, 16384], P(None, 'vol', 'dom'), may hold values from -6 to 6
- images: bfloat16 [8192, 16384], P(('dom', 'vol'))
- defocus: float32 [8192], P(('dom', 'vol')), may hold values from 0.5 to 3
- inv_noise: float32 [16384], replicated, may hold values from 0.004 to 0.04
- class_idx: int32 [8192, 4], P(('dom', 'vol')), may hold values from 0 to 3
- pose_idx: int32 [8192, 4], P(('dom', 'vol')), may hold values from 0 to 23
- slab_offset: int32 [24, 128], replicated, may hold values from -2048 to 2048, as said below
Outputs:
- weights: float32 [8192, 4], P(('dom', 'vol'))
- data_acc: bfloat16 [4, 256, 16384], P(None, 'vol', 'dom')
- weight_acc: bfloat16 [4, 256, 8192], P(None, 'vol', 'dom')
The draws below stay inside these ranges and needn't reach their ends.
Inputs may be any that keep to these rules, and one draw needn't show every extreme that they name: slab_offset[p, r] = t_p (r - 64) with integer tilts t_p of -32 to 32, both ends taken by some orientation.
All inputs are finite; a program needn't handle non-finite values.
Results may differ from the reference program's by a relative error of at most 0.012.
Values may be sent and summed in bfloat16 or wider, within the bound.
A program may use at most 128 MiB of HBM per device.

```python
import math
import jax
import jax.numpy as jnp
import numpy as np
from jax import lax

CLS = 4
NZ = 256
NY = 128
NXH = 64
NX2 = 128
POSES = 24
K = 4
CANDS = 96
NPART = 8192


def draw_images(key, part):
    first_key = jax.random.fold_in(key, 0)
    values = jax.random.normal(first_key, (NPART, NY * NX2), jnp.float32)
    return values.astype(jnp.bfloat16)


def draw_slab_offset(key, part):
    first_key, second_key, third_key = jax.random.split(key, 3)
    reach = 16 * NZ // NY
    tilts = jax.random.randint(first_key, (POSES,), -reach, reach + 1)
    first_pose = jax.random.randint(second_key, (), 0, POSES)
    second_pose = jnp.mod(first_pose + 1 + jax.random.randint(third_key, (), 0, POSES - 1), POSES)
    tilts = tilts.at[first_pose].set(-reach).at[second_pose].set(reach)
    rows = jnp.arange(NY, dtype=jnp.int32) - NY // 2
    return (tilts[:, None] * rows[None, :]).astype(jnp.int32)


def with_ends(entries, stream_key, least, high):
    place = [jax.random.randint(jax.random.fold_in(stream_key, axis), (), 0, length) for axis, length in enumerate(entries.shape)]
    main_axis = entries.shape.index(max(entries.shape))
    beside = place[:main_axis] + [(place[main_axis] + 1) % entries.shape[main_axis]] + place[main_axis + 1:]
    return entries.at[tuple(place)].set(least).at[tuple(beside)].set(high)


def levels(own_key, extent, pieces, low, high):
    level = 1.0
    for position, shards_of in pieces:
        heights = jax.random.uniform(jax.random.fold_in(jax.random.fold_in(own_key, 6), position), (shards_of,), jnp.float32, low / len(pieces), high / len(pieces))
        level = level * jnp.repeat(jnp.exp(heights), extent[position] // shards_of).reshape((-1,) + (1,) * (len(extent) - 1 - position))
    return level


def rank_bounds(count, lean):
    weights = [(1 << 20) // math.isqrt(rank ** lean) + 1 for rank in range(1, count + 1)]
    width = 1 + sum(weights) // (1 << 30)
    return np.cumsum(np.array([max(1, weight // width) for weight in weights]))


def ranked(key, shape, count, skew):
    grid = rank_bounds(count, skew)
    ticket = jax.random.randint(jax.random.fold_in(key, 1), shape, 0, int(grid[count - 1]))
    grade = jnp.searchsorted(jnp.asarray(grid, jnp.int32), ticket, side="right")
    return jax.random.permutation(jax.random.fold_in(key, 2), count)[grade].astype(jnp.int32)


def noise(stream_key, dims, deviation, limit, pieces=(), held_as=jnp.bfloat16):
    result = jax.random.normal(stream_key, dims, jnp.float32) * deviation
    if len(pieces) > 0:
        result = levels(stream_key, dims, pieces, -0.22, 0.18) * result
    return jnp.clip(result, min=-limit, max=limit).astype(held_as)


def setup_inputs(seed: int = 0) -> dict:
    keys = jax.random.split(jax.random.key(seed), 8)
    return {
        "volume": noise(keys[0], (CLS, NZ, NY * NX2), 1.0, 6.0, ((1, 8), (2, 16))),
        "images": draw_images(jax.random.fold_in(keys[7], 71), 0),
        "defocus": jnp.clip(jnp.exp(math.log(3.0) - 1.7917595 * jax.random.uniform(keys[2], (NPART,), jnp.float32) ** levels(keys[2], (NPART,), ((0, 128),), -0.2, 0.2)), 0.5, 3.0),
        "inv_noise": jnp.clip(jnp.exp(jax.random.uniform(keys[3], (NY * NX2,), jnp.float32, math.log(0.004), math.log(0.04))), 0.004, 0.04),
        "class_idx": with_ends(jax.random.randint(keys[4], (NPART, K), 0, CLS), jax.random.fold_in(keys[4], 1), 0, CLS - 1).astype(jnp.int32),
        "pose_idx": with_ends(ranked(keys[5], (NPART, K), POSES, 2), jax.random.fold_in(keys[5], 3), 0, POSES - 1).astype(jnp.int32),
        "slab_offset": draw_slab_offset(jax.random.fold_in(keys[7], 71), 0),
    }


def interp_matrix(offsets, slab_ids):
    integral = jnp.floor_divide(offsets, 16)
    lower_slab = jnp.mod(integral, NZ)
    upper_slab = jnp.mod(integral + 1, NZ)
    fraction = jnp.mod(offsets, 16).astype(jnp.float32) / 16.0
    return (jnp.where(lower_slab[..., None] == slab_ids, 1.0 - fraction[..., None], 0.0)
            + jnp.where(upper_slab[..., None] == slab_ids, fraction[..., None], 0.0)).astype(jnp.float32)


def frequency_squares():
    rows = jnp.arange(NY, dtype=jnp.int32)
    signed_rows = jnp.where(rows < NY // 2, rows, rows - NY)
    columns = jnp.mod(jnp.arange(NX2, dtype=jnp.int32), NXH)
    squares = signed_rows[:, None] ** 2 + columns[None, :] ** 2
    return (squares.astype(jnp.float32) / float((NY // 2) ** 2)).reshape(-1)


def reference(volume, images, defocus, inv_noise, class_idx, pose_idx, slab_offset):
    interp = interp_matrix(slab_offset, jnp.arange(NZ, dtype=jnp.int32))
    dense_vol = volume.astype(jnp.float32).reshape(CLS, NZ, NY, NX2)
    slices = jnp.einsum('prz,czrx->cprx', interp, dense_vol, precision=lax.Precision.HIGHEST)
    slices = slices.reshape(CANDS, NY * NX2).astype(jnp.bfloat16)
    squares = frequency_squares()
    block = math.gcd(NPART, 512)
    blocks = NPART // block
    cand_ids = (class_idx * POSES + pose_idx).astype(jnp.int32)

    def step(carry, inputs):
        data_sum, weight_sum = carry
        pictures, focus, chosen = inputs
        contrast = -jnp.sin(6.0 * focus[:, None] * squares[None, :] + 0.1)
        signal = contrast * pictures.astype(jnp.float32)
        looked = slices[chosen].astype(jnp.float32)
        contrast_sq = contrast * contrast
        scores = jnp.sum(inv_noise * (signal[:, None, :] * looked - 0.5 * contrast_sq[:, None, :] * looked * looked), axis=-1)
        probs = jax.nn.softmax(scores, axis=-1)
        contrib = (probs[:, :, None] * signal[:, None, :]).astype(jnp.bfloat16).reshape(-1, NY * NX2)
        half_sq = contrast_sq.reshape(-1, NY, NX2)[:, :, :NXH].reshape(-1, NY * NXH)
        ctf_sq = (probs[:, :, None] * half_sq[:, None, :]).astype(jnp.bfloat16).reshape(-1, NY * NXH)
        flat_ids = chosen.reshape(-1)
        data_sum = data_sum + jax.ops.segment_sum(contrib.astype(jnp.float32), flat_ids, CANDS)
        weight_sum = weight_sum + jax.ops.segment_sum(ctf_sq.astype(jnp.float32), flat_ids, CANDS)
        return (data_sum, weight_sum), probs

    start_carry = (jnp.zeros((CANDS, NY * NX2), jnp.float32), jnp.zeros((CANDS, NY * NXH), jnp.float32))
    inputs = (images.reshape(blocks, block, NY * NX2), defocus.reshape(blocks, block), cand_ids.reshape(blocks, block, K))
    (data_slices, weight_slices), probs = lax.scan(step, start_carry, inputs)
    weights = probs.reshape(NPART, K)
    data_acc = jnp.einsum('prz,cprx->czrx', interp, data_slices.reshape(CLS, POSES, NY, NX2), precision=lax.Precision.HIGHEST)
    weight_acc = jnp.einsum('prz,cprx->czrx', interp, weight_slices.reshape(CLS, POSES, NY, NXH), precision=lax.Precision.HIGHEST)
    return (weights,
            data_acc.reshape(CLS, NZ, NY * NX2).astype(jnp.bfloat16),
            weight_acc.reshape(CLS, NZ, NY * NXH).astype(jnp.bfloat16))
```

```python
import functools
import math

import jax
import jax.numpy as jnp
import numpy as np
from jax import lax
from jax.experimental import pallas as pl
from jax.experimental.pallas import tpu as pltpu
from jax.sharding import PartitionSpec as P

MESH = pl.DeviceIdType.MESH
F32 = jnp.float32
BF16 = jnp.bfloat16

CLS = 4
NZ = 256
NY = 128
NXH = 64
NX2 = 128
POSES = 24
K = 4
CANDS = 96
THIRD = 32
RING = 4
PLANE = 16


def sine_coefficients(terms):
    nodes = 0.5 * np.cos((np.arange(200) + 0.5) * math.pi / 400)
    table = np.stack([nodes ** (2 * k + 1) for k in range(terms)], axis=1)
    return np.linalg.lstsq(table, np.sin(2 * math.pi * nodes), rcond=None)[0].tolist()


SINE = sine_coefficients(5)
ROUNDER = 12582912.0


def sine_of_turns(turns):
    rest = turns - ((turns + ROUNDER) - ROUNDER)
    square = rest * rest
    value = SINE[-1] * square + SINE[-2]
    for coefficient in SINE[-3::-1]:
        value = value * square + coefficient
    return value * rest


def nt_dot(left, right):
    return lax.dot_general(left, right, (((1,), (1,)), ((), ())), preferred_element_type=F32)


def dot(left, right):
    return jnp.dot(left, right, preferred_element_type=F32)


def kernel(
    volume, images, defocus, inv_noise, class_idx, pose_idx, slab_offset,
    weights_out, data_out, weight_out,
    imgs, signal, scaled, quad, focus,
    volrow, back,
    meta_own, meta_sib, meta_all,
    sl_a, sl_b, sl_c,
    part_own, part_sib,
    w_all, ctf_sq,
    rs_a, rs_b, rs_c, in_a, in_b, in_c, sum_a, sum_b, sum_c, fin_a, fin_b, fin_c,
    data_send, w_send, w_recv,
    local_sem, sib_send, sib_recv, vol_send, vol_recv, meta_send, meta_recv,
    ag_send, ag_recv, ring_send, ring_recv, w_sems, rs_send, rs_recv, fin_send, fin_recv,
    out_send, out_recv,
):
    dom = lax.axis_index("dom")
    vol = lax.axis_index("vol")
    x = (dom // 8) * 2 + vol % 2
    y = (dom // 2) % 4
    z = vol // 2
    c = dom % 2
    row = dom * 8 + vol

    def device(px, py, pz, pc):
        return ((px // 2) * 8 + py * 2 + pc, pz * 2 + px % 2)

    def near(dx, dy, dz):
        return (x + dx) % 4, (y + dy) % 4, (z + dz) % 4

    def send(src, dst, send_sem, recv_sem, target):
        pltpu.make_async_remote_copy(
            src_ref=src, dst_ref=dst, send_sem=send_sem, recv_sem=recv_sem,
            device_id=target, device_id_type=MESH,
        ).start()

    def wait(ref, sem):
        pltpu.make_async_copy(ref, ref, sem).wait()

    sibling = device(x, y, z, 1 - c)

    partners = [
        (dx, dy, dz)
        for dx in range(4) for dy in range(4) for dz in range(4)
        if (dx, dy, dz) != (0, 0, 0) and 0 in (dx, dy, dz)
    ]
    barrier = pltpu.get_barrier_semaphore()
    pl.semaphore_signal(barrier, inc=1, device_id=sibling, device_id_type=MESH)
    for dx, dy, dz in partners:
        pl.semaphore_signal(barrier, inc=1, device_id=device(*near(dx, dy, dz), c), device_id_type=MESH)

    def own_images(b):
        return images.at[:, pl.ds(pl.multiple_of((2 * b + c) * 1024, 1024), 1024)]

    def other_images(b):
        return images.at[:, pl.ds(pl.multiple_of((2 * b + 1 - c) * 1024, 1024), 1024)]

    mine = pl.ds(pl.multiple_of(c * 64, 64), 64)
    own_lanes = pl.ds(pl.multiple_of(vol * 128, 128), 128)
    for b in range(8):
        pltpu.make_async_copy(own_images(b), imgs.at[b, mine], local_sem.at[0]).start()
    pltpu.make_async_copy(volume.at[:, :, own_lanes], volrow.at[vol], local_sem.at[1]).start()

    lane64 = lax.broadcasted_iota(jnp.int32, (64, 128), 1)
    pair = (class_idx[...] * POSES + pose_idx[...]).astype(F32)
    wide = jnp.zeros((64, 128), F32)
    for k in range(K):
        wide = jnp.where(lane64 == k, pair[:, k : k + 1], wide)
    ids = jnp.transpose(jnp.concatenate([wide, jnp.zeros((64, 128), F32)], axis=0))[0:8]
    sub8 = lax.broadcasted_iota(jnp.int32, (8, 128), 0)
    lane8 = lax.broadcasted_iota(jnp.int32, (8, 128), 1)
    focus_row = jnp.concatenate([defocus[...], jnp.zeros((1, 64), F32)], axis=1)
    meta_own[...] = jnp.where(sub8 == 4, focus_row, ids)

    lane24 = lax.broadcasted_iota(jnp.int32, (POSES, 128), 1)
    offset = jnp.sum(jnp.where(lane24 == row, slab_offset[...].astype(F32), 0.0), axis=1, keepdims=True)
    offset = offset.astype(jnp.int32)
    whole = lax.shift_right_arithmetic(offset, 4)
    lower = lax.bitwise_and(whole, NZ - 1)
    upper = lax.bitwise_and(whole + 1, NZ - 1)
    fraction = lax.bitwise_and(offset, 15).astype(F32) * (1.0 / 16.0)
    slab = lax.broadcasted_iota(jnp.int32, (POSES, NZ), 1)
    interp = jnp.where(slab == lower, 1.0 - fraction, 0.0) + jnp.where(slab == upper, fraction, 0.0)
    padded = jnp.concatenate([interp, interp, jnp.zeros((128 - 2 * POSES, NZ), F32)], axis=0)
    back[...] = jnp.transpose(padded).astype(BF16)

    pl.semaphore_wait(barrier, len(partners) + 1)

    for dz in range(4):
        for dxl in range(2):
            if dz == 0 and dxl == 0:
                continue
            pz = (z + dz) % 4
            pv = pz * 2 + (vol + dxl) % 2
            send(
                volume.at[:, :, pl.ds(pl.multiple_of(pv * 128, 128), 128)], volrow.at[vol],
                vol_send, vol_recv, (dom, pv),
            )
    send(meta_own, meta_sib, sib_send.at[0], sib_recv.at[0], sibling)
    for b in range(8):
        send(other_images(b), imgs.at[b, mine], sib_send.at[1], sib_recv.at[1], sibling)

    wait(meta_sib, sib_recv.at[0])
    first = jnp.where(c == 0, meta_own[...], meta_sib[...])
    second = jnp.where(c == 0, meta_sib[...], meta_own[...])
    meta = jnp.where(lane8 < 64, first, pltpu.roll(second, 64, 1))
    plane_yz = y * 4 + z
    plane_xz = x * 4 + z
    plane_xy = x * 4 + y
    meta_all[x, plane_yz] = meta
    for j in range(1, PLANE):
        px, py, pz = near(0, j // 4, j % 4)
        send(
            meta_all.at[x, plane_yz], meta_all.at[x, plane_yz],
            meta_send.at[0], meta_recv.at[0], device(px, py, pz, c),
        )
    columns = jnp.transpose(jnp.concatenate([meta, jnp.zeros((120, 128), F32)], axis=0))
    focus[...] = jnp.broadcast_to(columns[:, 4:5], (128, 128))

    lane_row = lax.broadcasted_iota(jnp.int32, (1, 128), 1) % NXH
    kx_sq = (lane_row * lane_row).astype(F32)
    turn = 6.0 / (2.0 * math.pi * (NY // 2) ** 2)

    def prepare(step, carry):
        b = step // 8
        v = step % 8
        r = (2 * b + c) * 8 + v
        ky = jnp.where(r < NY // 2, r, r - NY)
        squares = (kx_sq + (ky * ky).astype(F32)) * turn
        lanes = pl.ds(pl.multiple_of(v * 128, 128), 128)
        contrast = -sine_of_turns(focus[...] * squares + 0.1 / (2.0 * math.pi))
        seen = contrast * imgs[b, :, lanes].astype(F32)
        noise = inv_noise[pl.ds(r, 1), :]
        signal[b, :, lanes] = seen.astype(BF16)
        scaled[b, :, lanes] = (seen * noise).astype(BF16)
        quad[b, :, lanes] = (contrast * contrast * (-0.5 * noise)).astype(BF16)
        return carry

    wait(volrow.at[0], local_sem.at[1])
    wait(volrow.at[0:7], vol_recv)
    narrow = interp.astype(BF16)
    rows = [
        dot(narrow, jnp.concatenate([volrow[j, g] for j in range(8)], axis=0)) for g in range(CLS)
    ]
    slices = jnp.concatenate(rows, axis=0).astype(BF16)
    sl_a[x, plane_yz] = slices[0:THIRD]
    sl_b[y, plane_xz] = slices[THIRD : 2 * THIRD]
    sl_c[z, plane_xy] = slices[2 * THIRD :]
    for j in range(1, PLANE):
        spot = sl_a.at[x, plane_yz]
        send(spot, spot, ag_send, ag_recv.at[0], device(*near(0, j // 4, j % 4), c))
        spot = sl_b.at[y, plane_xz]
        send(spot, spot, ag_send, ag_recv.at[1], device(*near(j // 4, 0, j % 4), c))
        spot = sl_c.at[z, plane_xy]
        send(spot, spot, ag_send, ag_recv.at[2], device(*near(j // 4, j % 4, 0), c))

    wait(imgs.at[:, 0:64], local_sem.at[0])
    wait(imgs.at[:, 0:64], sib_recv.at[1])
    lax.fori_loop(0, 64, prepare, 0)

    for d in range(1, 4):
        wait_for = meta_all.at[0, 0:15]
        if d == 1:
            wait(wait_for, meta_recv.at[0])
        send(meta_all.at[x], meta_all.at[x], meta_send.at[1], meta_recv.at[1], device(*near(d, 0, 0), c))
    wait(sl_a.at[0, 0:15], ag_recv.at[0])
    for d in range(1, 4):
        send(sl_a.at[x], sl_a.at[x], ring_send, ring_recv.at[0], device(*near(d, 0, 0), c))
    wait(sl_b.at[0, 0:15], ag_recv.at[1])
    for d in range(1, 4):
        send(sl_b.at[y], sl_b.at[y], ring_send, ring_recv.at[1], device(*near(0, d, 0), c))
    wait(sl_c.at[0, 0:15], ag_recv.at[2])
    for d in range(1, 4):
        send(sl_c.at[z], sl_c.at[z], ring_send, ring_recv.at[2], device(*near(0, 0, d), c))

    wait(meta_all.at[0:3], meta_recv.at[1])
    own_ky = jnp.where(row < NY // 2, row, row - NY)
    sub64 = lax.broadcasted_iota(jnp.int32, (NXH, 128), 0)
    own_squares = (sub64 * sub64 + own_ky * own_ky).astype(F32) * turn

    def square_row(step, carry):
        px = step // PLANE
        pp = step % PLANE
        wave = sine_of_turns(meta_all[px, pp, 4:5, :] * own_squares + 0.1 / (2.0 * math.pi))
        ctf_sq[step] = (wave * wave).astype(BF16)
        return carry

    lax.fori_loop(0, 64, square_row, 0)

    wait(sl_a.at[0:3], ring_recv.at[0])
    wait(sl_b.at[0:3], ring_recv.at[1])
    wait(sl_c.at[0:3], ring_recv.at[2])

    def score_band(b, total):
        pieces = []
        py = b % 4
        for v in range(8):
            px = (b // 4) * 2 + v % 2
            pz = v // 2
            pieces.append(
                jnp.concatenate(
                    [sl_a[px, py * 4 + pz], sl_b[py, px * 4 + pz], sl_c[pz, px * 4 + py]], axis=0
                )
            )
        band = jnp.concatenate(pieces, axis=1)
        wide_band = band.astype(F32)
        band_sq = (wide_band * wide_band).astype(BF16)
        return total + nt_dot(band, scaled[b]) + nt_dot(band_sq, quad[b])

    scores = lax.fori_loop(0, 8, score_band, jnp.zeros((CANDS, 128), F32))
    sub96 = lax.broadcasted_iota(jnp.int32, (CANDS, 128), 0).astype(F32)
    picked = [
        jnp.sum(jnp.where(sub96 == meta[k : k + 1], scores, 0.0), axis=0, keepdims=True) for k in range(K)
    ]
    part_own[...] = jnp.concatenate(picked + [jnp.zeros((4, 128), F32)], axis=0)
    send(part_own, part_sib, sib_send.at[2], sib_recv.at[2], sibling)
    wait(part_sib, sib_recv.at[2])
    both = (part_own[...] + part_sib[...])[0:K]
    best = jnp.max(both, axis=0, keepdims=True)
    grown = jnp.exp(both - best)
    weights = grown / jnp.sum(grown, axis=0, keepdims=True)
    w_all[x, plane_yz] = weights
    for j in range(1, PLANE):
        spot = w_all.at[x, plane_yz]
        send(spot, spot, w_sems.at[0], w_sems.at[1], device(*near(0, j // 4, j % 4), c))

    spread = jnp.zeros((CANDS, 128), F32)
    for k in range(K):
        spread = spread + jnp.where(sub96 == meta[k : k + 1], weights[k : k + 1], 0.0)
    spread = spread.astype(BF16)

    def sum_band(b, carry):
        band = dot(spread, signal[b]).astype(BF16)
        py = b % 4
        for v in range(8):
            px = (b // 4) * 2 + v % 2
            pz = v // 2
            piece = band[:, v * 128 : (v + 1) * 128]
            rs_a[px, py * 4 + pz] = piece[0:THIRD]
            rs_b[py, px * 4 + pz] = piece[THIRD : 2 * THIRD]
            rs_c[pz, px * 4 + py] = piece[2 * THIRD :]
        return carry

    lax.fori_loop(0, 8, sum_band, 0)
    for d in (2, 1, 3):
        px, py, pz = near(d, d, d)
        send(rs_a.at[px], in_a.at[d - 1], rs_send, rs_recv.at[0], device(px, y, z, c))
        send(rs_b.at[py], in_b.at[d - 1], rs_send, rs_recv.at[1], device(x, py, z, c))
        send(rs_c.at[pz], in_c.at[d - 1], rs_send, rs_recv.at[2], device(x, y, pz, c))

    wait(w_all.at[0, 0:15], w_sems.at[1])
    for d in range(1, 4):
        send(w_all.at[x], w_all.at[x], w_sems.at[2], w_sems.at[3], device(*near(d, 0, 0), c))

    whole_weights = jnp.transpose(jnp.concatenate([weights, jnp.zeros((124, 128), F32)], axis=0))
    weights_out[...] = jnp.where(c == 0, whole_weights[0:64], whole_weights[64:128])[:, 0:K]

    def ring_sum(mine_ref, in_ref, sum_ref, place):
        def step(i, carry):
            sum_ref[i] = (
                mine_ref[place, i].astype(F32) + in_ref[0, i].astype(F32)
                + in_ref[1, i].astype(F32) + in_ref[2, i].astype(F32)
            ).astype(BF16)
            return carry

        lax.fori_loop(0, PLANE, step, 0, unroll=4)

    wait(in_a, rs_recv.at[0])
    ring_sum(rs_a, in_a, sum_a, x)
    for j in range(1, PLANE):
        px, py, pz = near(0, j // 4, j % 4)
        send(sum_a.at[py * 4 + pz], fin_a.at[j - 1], fin_send, fin_recv.at[0], device(px, py, pz, c))
    wait(in_b, rs_recv.at[1])
    ring_sum(rs_b, in_b, sum_b, y)
    for j in range(1, PLANE):
        px, py, pz = near(j // 4, 0, j % 4)
        send(sum_b.at[px * 4 + pz], fin_b.at[j - 1], fin_send, fin_recv.at[1], device(px, py, pz, c))
    wait(in_c, rs_recv.at[2])
    ring_sum(rs_c, in_c, sum_c, z)
    for j in range(1, PLANE):
        px, py, pz = near(j // 4, j % 4, 0)
        send(sum_c.at[px * 4 + py], fin_c.at[j - 1], fin_send, fin_recv.at[2], device(px, py, pz, c))

    wait(w_all.at[0:3], w_sems.at[3])
    sub96w = lax.broadcasted_iota(jnp.int32, (CANDS, 128), 0).astype(F32)

    def weigh(step, total):
        px = step // PLANE
        pp = step % PLANE
        block = jnp.zeros((CANDS, 128), F32)
        for k in range(K):
            block = block + jnp.where(
                sub96w == meta_all[px, pp, k : k + 1, :], w_all[px, pp, k : k + 1, :], 0.0
            )
        return total + nt_dot(block.astype(BF16), ctf_sq[step])

    weight_slices = lax.fori_loop(0, 64, weigh, jnp.zeros((CANDS, NXH), F32))

    def backproject(sums, width):
        flat = jnp.concatenate([sums[g * POSES : (g + 1) * POSES] for g in range(CLS)], axis=1)
        high = flat.astype(BF16).astype(F32)
        stacked = jnp.concatenate(
            [high, flat - high, jnp.zeros((128 - 2 * POSES, CLS * width), F32)], axis=0
        )
        return dot(back[...], stacked.astype(BF16)).astype(BF16)

    result = backproject(weight_slices, NXH)
    for j in range(8):
        w_send[j] = result[j * 32 : (j + 1) * 32]
    w_recv[vol] = w_send[vol]
    for dz in range(4):
        for dxl in range(2):
            if dz == 0 and dxl == 0:
                continue
            pv = ((z + dz) % 4) * 2 + (vol + dxl) % 2
            send(w_send.at[pv], w_recv.at[vol], out_send.at[0], out_recv.at[0], (dom, pv))

    wait(fin_a, fin_recv.at[0])
    wait(fin_b, fin_recv.at[1])
    wait(fin_c, fin_recv.at[2])

    def final_sum(sum_ref, fin_ref, place):
        total = sum_ref[place].astype(F32)
        for j in range(PLANE - 1):
            total = total + fin_ref[j].astype(F32)
        return total

    own = jnp.concatenate(
        [final_sum(sum_a, fin_a, plane_yz), final_sum(sum_b, fin_b, plane_xz), final_sum(sum_c, fin_c, plane_xy)],
        axis=0,
    )
    result = backproject(own, NX2)
    for j in range(8):
        for g in range(CLS):
            data_send[j, g] = result[j * 32 : (j + 1) * 32, g * 128 : (g + 1) * 128]
    for dz in range(4):
        for dxl in range(2):
            if dz == 0 and dxl == 0:
                continue
            pv = ((z + dz) % 4) * 2 + (vol + dxl) % 2
            send(data_send.at[pv], data_out.at[:, :, own_lanes], out_send.at[1], out_recv.at[1], (dom, pv))
    keep = pltpu.make_async_copy(data_send.at[vol], data_out.at[:, :, own_lanes], local_sem.at[2])
    keep.start()

    wait(w_recv.at[0:7], out_recv.at[0])
    for pair_of in range(4):
        even = w_recv[2 * pair_of].astype(F32)
        odd = w_recv[2 * pair_of + 1].astype(F32)
        for g in range(CLS):
            lanes = slice(g * NXH, (g + 1) * NXH)
            weight_out[g, :, pair_of * 128 : (pair_of + 1) * 128] = jnp.concatenate(
                [even[:, lanes], odd[:, lanes]], axis=1
            ).astype(BF16)

    wait(meta_own, sib_send.at[0])
    wait(imgs.at[:, 0:64], sib_send.at[1])
    wait(part_own, sib_send.at[2])
    wait(volrow.at[0:7], vol_send)
    wait(meta_all.at[0, 0:15], meta_send.at[0])
    wait(meta_all.at[0:3], meta_send.at[1])
    wait(sl_a.at[0, 0:15], ag_send)
    wait(sl_b.at[0, 0:15], ag_send)
    wait(sl_c.at[0, 0:15], ag_send)
    wait(sl_a.at[0:3], ring_send)
    wait(sl_b.at[0:3], ring_send)
    wait(sl_c.at[0:3], ring_send)
    wait(w_all.at[0, 0:15], w_sems.at[0])
    wait(w_all.at[0:3], w_sems.at[2])
    wait(in_a, rs_send)
    wait(in_b, rs_send)
    wait(in_c, rs_send)
    wait(fin_a, fin_send)
    wait(fin_b, fin_send)
    wait(fin_c, fin_send)
    wait(w_recv.at[0:7], out_send.at[0])
    wait(data_send.at[0:7], out_send.at[1])
    keep.wait()
    wait(data_send.at[0:7], out_recv.at[1])


def body(volume, images, defocus, inv_noise, class_idx, pose_idx, slab_offset):
    vmem = pl.BlockSpec(memory_space=pltpu.VMEM)
    anywhere = pl.BlockSpec(memory_space=pl.ANY)
    dma = pltpu.SemaphoreType.DMA
    V = pltpu.VMEM
    block = (RING, PLANE, THIRD, 128)
    return pl.pallas_call(
        kernel,
        out_shape=(
            jax.ShapeDtypeStruct((64, K), F32),
            jax.ShapeDtypeStruct((CLS, 32, 1024), BF16),
            jax.ShapeDtypeStruct((CLS, 32, 512), BF16),
        ),
        in_specs=[anywhere, anywhere, vmem, vmem, vmem, vmem, vmem],
        out_specs=(vmem, anywhere, vmem),
        scratch_shapes=[
            V((8, 128, 1024), BF16), V((8, 128, 1024), BF16), V((8, 128, 1024), BF16),
            V((8, 128, 1024), BF16), V((128, 128), F32),
            V((8, CLS, 32, 128), BF16), V((NZ, 128), BF16),
            V((8, 128), F32), V((8, 128), F32), V((RING, PLANE, 8, 128), F32),
            V(block, BF16), V(block, BF16), V(block, BF16),
            V((8, 128), F32), V((8, 128), F32),
            V((RING, PLANE, K, 128), F32), V((64, NXH, 128), BF16),
            V(block, BF16), V(block, BF16), V(block, BF16),
            V((3, PLANE, THIRD, 128), BF16), V((3, PLANE, THIRD, 128), BF16), V((3, PLANE, THIRD, 128), BF16),
            V((PLANE, THIRD, 128), BF16), V((PLANE, THIRD, 128), BF16), V((PLANE, THIRD, 128), BF16),
            V((PLANE - 1, THIRD, 128), BF16), V((PLANE - 1, THIRD, 128), BF16), V((PLANE - 1, THIRD, 128), BF16),
            V((8, CLS, 32, 128), BF16), V((8, 32, CLS * NXH), BF16), V((8, 32, CLS * NXH), BF16),
            dma((3,)), dma((3,)), dma((3,)), dma, dma, dma((2,)), dma((2,)),
            dma, dma((3,)), dma, dma((3,)), dma((4,)), dma, dma((3,)), dma, dma((3,)),
            dma((2,)), dma((2,)),
        ],
        compiler_params=pltpu.CompilerParams(
            collective_id=0, has_side_effects=True, vmem_limit_bytes=40 * 2**20
        ),
    )(
        volume, images, defocus.reshape(1, 64), inv_noise.reshape(NY, NX2),
        class_idx, pose_idx, slab_offset,
    )


def solution(mesh):
    return jax.shard_map(
        body,
        mesh=mesh,
        in_specs=(
            P(None, "vol", "dom"),
            P(("dom", "vol"), None),
            P(("dom", "vol")),
            P(),
            P(("dom", "vol"), None),
            P(("dom", "vol"), None),
            P(),
        ),
        out_specs=(P(("dom", "vol"), None), P(None, "vol", "dom"), P(None, "vol", "dom")),
        check_vma=False,
    )
```

```python
import functools
import math

import jax
import jax.numpy as jnp
import numpy as np
from jax import lax
from jax.experimental import pallas as pl
from jax.experimental.pallas import tpu as pltpu
from jax.sharding import PartitionSpec as P

MESH = pl.DeviceIdType.MESH
F32 = jnp.float32
BF16 = jnp.bfloat16

CLS = 4
NZ = 256
NY = 128
NXH = 64
NX2 = 128
POSES = 24
K = 4
CANDS = 96
THIRD = 32
RING = 4
PLANE = 16

PLACES = (
    (0, 0), (0, 1), (0, 3), (1, 0), (3, 0),
    (0, 2), (2, 0), (1, 1), (1, 3), (3, 1), (3, 3),
    (1, 2), (3, 2), (2, 1), (2, 3), (2, 2),
)
PLACE_OF = {step: i for i, step in enumerate(PLACES)}
BACK_OF = [PLACE_OF[(-a) % 4, (-b) % 4] for a, b in PLACES]
CLASSES = ((0, 5), (5, 11), (11, 16))
CLASS_OF = [0] * 5 + [1] * 6 + [2] * 5


def around(axis, turn, place):
    first, second = PLACES[place]
    return ((turn, first, second), (first, turn, second), (first, second, turn))[axis]


def sine_coefficients(terms):
    nodes = 0.5 * np.cos((np.arange(200) + 0.5) * math.pi / 400)
    table = np.stack([nodes ** (2 * k + 1) for k in range(terms)], axis=1)
    return np.linalg.lstsq(table, np.sin(2 * math.pi * nodes), rcond=None)[0].tolist()


SINE = sine_coefficients(5)
ROUNDER = 12582912.0


def sine_of_turns(turns):
    rest = turns - ((turns + ROUNDER) - ROUNDER)
    square = rest * rest
    value = SINE[-1] * square + SINE[-2]
    for coefficient in SINE[-3::-1]:
        value = value * square + coefficient
    return value * rest


def nt_dot(left, right):
    return lax.dot_general(left, right, (((1,), (1,)), ((), ())), preferred_element_type=F32)


def dot(left, right):
    return jnp.dot(left, right, preferred_element_type=F32)


def kernel(
    volume, images, defocus, inv_noise, class_idx, pose_idx, slab_offset,
    weights_out, data_out, weight_out,
    focus_in, noise, cls_in, pose_in, slab_in,
    imgs, signal, scaled, quad, focus,
    volrow, back,
    meta_own, meta_sib, meta_all,
    sl,
    part_own, part_sib,
    w_all, ctf_sq,
    parts, incoming, sums, last,
    data_send, w_send, w_recv, w_held, sq_held,
    local_sem, sib_send, sib_recv, vol_send, vol_recv, meta_send, meta_recv,
    ag_send, ag_recv, ring_send, ring_recv, w_send_sem, w_recv_sem, rs_send, rs_recv, fin_send, fin_recv,
    out_send, out_recv,
):
    dom = lax.axis_index("dom")
    vol = lax.axis_index("vol")
    x = (dom // 8) * 2 + vol % 2
    y = (dom // 2) % 4
    z = vol // 2
    c = dom % 2
    row = dom * 8 + vol

    def device(px, py, pz, pc):
        return ((px // 2) * 8 + py * 2 + pc, pz * 2 + px % 2)

    def near(dx, dy, dz):
        return (x + dx) % 4, (y + dy) % 4, (z + dz) % 4

    def send(src, dst, send_sem, recv_sem, target):
        pltpu.make_async_remote_copy(
            src_ref=src, dst_ref=dst, send_sem=send_sem, recv_sem=recv_sem,
            device_id=target, device_id_type=MESH,
        ).start()

    under_way = {}

    def due(ref, sem):
        name = object()
        under_way[name] = (ref, sem)

        def now():
            del under_way[name]
            pltpu.make_async_copy(ref, ref, sem).wait()

        return now

    def load(src, dst, sem):
        pltpu.make_async_copy(src, dst, sem).start()
        return due(dst, sem)

    sibling = device(x, y, z, 1 - c)

    def at(steps):
        return device(*near(*steps), c)

    barrier = pltpu.get_barrier_semaphore()
    pl.semaphore_signal(barrier, inc=1, device_id=sibling, device_id_type=MESH)
    for k in range(1, 8):
        pl.semaphore_signal(barrier, inc=1, device_id=(dom, (vol + k) % 8), device_id_type=MESH)
        pl.semaphore_signal(barrier, inc=1, device_id=((dom + 2 * k) % 16, vol), device_id_type=MESH)

    def own_images(b):
        return images.at[:, pl.ds(pl.multiple_of((2 * b + c) * 1024, 1024), 1024)]

    def other_images(b):
        return images.at[:, pl.ds(pl.multiple_of((2 * b + 1 - c) * 1024, 1024), 1024)]

    mine = pl.ds(pl.multiple_of(c * 64, 64), 64)
    own_lanes = pl.ds(pl.multiple_of(vol * 128, 128), 128)
    small = [
        load(class_idx, cls_in, local_sem.at[3]),
        load(pose_idx, pose_in, local_sem.at[4]),
        load(defocus, focus_in, local_sem.at[5]),
        load(slab_offset, slab_in, local_sem.at[6]),
        load(inv_noise, noise, local_sem.at[7]),
    ]
    own_volume = load(volume.at[:, :, own_lanes], volrow.at[vol], local_sem.at[1])
    for b in range(8):
        pltpu.make_async_copy(own_images(b), imgs.at[b, mine], local_sem.at[0]).start()
    local_images = due(imgs.at[:, 0:64], local_sem.at[0])
    for arrived in small:
        arrived()

    pair = (cls_in[...] * POSES + pose_in[...]).astype(F32)
    meta_own[...] = jnp.concatenate(
        [jnp.concatenate([pair, focus_in[...], jnp.zeros((3, 64), F32)], axis=0), jnp.zeros((8, 64), F32)], axis=1
    )

    lane24 = lax.broadcasted_iota(jnp.int32, (POSES, 128), 1)
    offset = jnp.sum(jnp.where(lane24 == row, slab_in[...].astype(F32), 0.0), axis=1, keepdims=True)
    offset = offset.astype(jnp.int32)
    whole = lax.shift_right_arithmetic(offset, 4)
    lower = lax.bitwise_and(whole, NZ - 1)
    upper = lax.bitwise_and(whole + 1, NZ - 1)
    fraction = lax.bitwise_and(offset, 15).astype(F32) * (1.0 / 16.0)
    slab = lax.broadcasted_iota(jnp.int32, (POSES, NZ), 1)
    interp = jnp.where(slab == lower, 1.0 - fraction, 0.0) + jnp.where(slab == upper, fraction, 0.0)
    padded = jnp.concatenate([interp, interp, jnp.zeros((128 - 2 * POSES, NZ), F32)], axis=0)
    back[...] = jnp.transpose(padded).astype(BF16)

    pl.semaphore_wait(barrier, 15)

    vol_steps = ((2, 1), (1, 1), (3, 1), (2, 0), (1, 0), (3, 0), (0, 1))
    members = [((z + dz) % 4) * 2 + (vol + dx) % 2 for dz, dx in vol_steps]
    for pv in members:
        send(
            volume.at[:, :, pl.ds(pl.multiple_of(pv * 128, 128), 128)], volrow.at[vol],
            vol_send, vol_recv, (dom, pv),
        )
    volume_rows = due(volrow.at[0:7], vol_recv)
    due(volrow.at[0:7], vol_send)
    send(meta_own, meta_sib, sib_send.at[0], sib_recv.at[0], sibling)
    sibling_meta = due(meta_sib, sib_recv.at[0])
    due(meta_own, sib_send.at[0])
    for b in range(8):
        send(other_images(b), imgs.at[b, mine], sib_send.at[1], sib_recv.at[1], sibling)
    sibling_images = due(imgs.at[:, 0:64], sib_recv.at[1])
    due(imgs.at[:, 0:64], sib_send.at[1])

    sibling_meta()
    lane8 = lax.broadcasted_iota(jnp.int32, (8, 128), 1)
    first = jnp.where(c == 0, meta_own[...], meta_sib[...])
    second = jnp.where(c == 0, meta_sib[...], meta_own[...])
    meta = jnp.where(lane8 < 64, first, pltpu.roll(second, 64, 1))
    meta_all[0] = meta
    columns = jnp.transpose(jnp.concatenate([meta, jnp.zeros((120, 128), F32)], axis=0))
    focus[...] = jnp.broadcast_to(columns[:, 4:5], (128, 128))

    lane_row = lax.broadcasted_iota(jnp.int32, (1, 128), 1) % NXH
    kx_sq = (lane_row * lane_row).astype(F32)
    turn = 6.0 / (2.0 * math.pi * (NY // 2) ** 2)

    def prepare(step, carry):
        px, py, pz = near(step // 16, (step // 4) % 4, step % 4)
        b = (px // 2) * 4 + py
        v = pz * 2 + px % 2
        r = (2 * b + c) * 8 + v
        ky = jnp.where(r < NY // 2, r, r - NY)
        squares = (kx_sq + (ky * ky).astype(F32)) * turn
        lanes = pl.ds(pl.multiple_of(v * 128, 128), 128)
        group = step // 8
        spot = pl.ds(pl.multiple_of((step % 8) * 128, 128), 128)
        contrast = -sine_of_turns(focus[...] * squares + 0.1 / (2.0 * math.pi))
        seen = contrast * imgs[b, :, lanes].astype(F32)
        level = noise[pl.ds(r, 1), :]
        signal[group, :, spot] = seen.astype(BF16)
        scaled[group, :, spot] = (seen * level).astype(BF16)
        quad[group, :, spot] = (contrast * contrast * (-0.5 * level)).astype(BF16)
        return carry

    local_images()
    sibling_images()
    lax.fori_loop(0, 24, prepare, 0)

    own_volume()
    volume_rows()
    narrow = interp.astype(BF16)
    rows = [
        dot(narrow, jnp.concatenate([volrow[j, g] for j in range(8)], axis=0)) for g in range(CLS)
    ]
    slices = jnp.concatenate(rows, axis=0).astype(BF16)
    for t in range(3):
        sl[t, 0, 0] = slices[t * THIRD : (t + 1) * THIRD]
    for place in (*range(1, 5), *range(15, 4, -1)):
        for t in range(3):
            send(
                sl.at[t, 0, 0], sl.at[t, 0, BACK_OF[place]],
                ag_send, ag_recv.at[t, CLASS_OF[place]], at(around(t, 0, place)),
            )
    planes = [
        [due(sl.at[t, 0, max(low, 1) : high], ag_recv.at[t, i]) for t in range(3)]
        for i, (low, high) in enumerate(CLASSES)
    ]
    due(sl.at[:, 0, 0:15], ag_send)
    lax.fori_loop(24, 44, prepare, 0)

    for i, (low, high) in enumerate(CLASSES):
        for t in range(3):
            planes[i][t]()
            for d in (2, 1, 3):
                send(
                    sl.at[t, 0, low:high], sl.at[t, 4 - d, low:high],
                    ring_send, ring_recv.at[t], at(around(t, d, 0)),
                )
    rest = [due(sl.at[t, 1:4], ring_recv.at[t]) for t in range(3)]
    due(sl.at[:, 1:4], ring_send)
    lax.fori_loop(44, 64, prepare, 0)

    for arrived in rest:
        arrived()

    scores = jnp.zeros((CANDS, 128), F32)
    for group in range(8):
        pieces = []
        for step in range(8 * group, 8 * group + 8):
            dx, dy, dz = step // 16, (step // 4) % 4, step % 4
            pieces.append(
                jnp.concatenate(
                    [
                        sl[0, dx, PLACE_OF[dy, dz]],
                        sl[1, dy, PLACE_OF[dx, dz]],
                        sl[2, dz, PLACE_OF[dx, dy]],
                    ],
                    axis=0,
                )
            )
        band = jnp.concatenate(pieces, axis=1)
        wide_band = band.astype(F32)
        band_sq = (wide_band * wide_band).astype(BF16)
        scores = scores + nt_dot(band, scaled[group]) + nt_dot(band_sq, quad[group])
    sub96 = lax.broadcasted_iota(jnp.int32, (CANDS, 128), 0).astype(F32)
    picked = [
        jnp.sum(jnp.where(sub96 == meta[k : k + 1], scores, 0.0), axis=0, keepdims=True) for k in range(K)
    ]
    part_own[...] = jnp.concatenate(picked + [jnp.zeros((4, 128), F32)], axis=0)
    send(part_own, part_sib, sib_send.at[2], sib_recv.at[2], sibling)
    due(part_own, sib_send.at[2])
    sibling_part = due(part_sib, sib_recv.at[2])
    for place in range(PLANE - 1, -1, -1):
        for d in (2, 1, 3, 0):
            if (d, place) != (0, 0):
                send(
                    meta_all.at[0], meta_all.at[(4 - d) % 4 * PLANE + BACK_OF[place]],
                    meta_send, meta_recv, at(around(0, d, place)),
                )
    due(meta_all.at[0:63], meta_send)
    every_meta = due(meta_all.at[0:63], meta_recv)
    sibling_part()
    both = (part_own[...] + part_sib[...])[0:K]
    best = jnp.max(both, axis=0, keepdims=True)
    grown = jnp.exp(both - best)
    weights = grown / jnp.sum(grown, axis=0, keepdims=True)
    w_all[0] = weights
    w_held[...] = jnp.where(c == 0, weights, pltpu.roll(weights, 64, 1))[:, 0:64]
    load(w_held, weights_out, local_sem.at[8])

    spread = jnp.zeros((CANDS, 128), F32)
    for k in range(K):
        spread = spread + jnp.where(sub96 == meta[k : k + 1], weights[k : k + 1], 0.0)
    spread = spread.astype(BF16)

    for group in range(8):
        band = dot(spread, signal[group]).astype(BF16)
        for i in range(8):
            step = 8 * group + i
            dx, dy, dz = step // 16, (step // 4) % 4, step % 4
            piece = band[:, i * 128 : (i + 1) * 128]
            parts[0, dx, PLACE_OF[dy, dz]] = piece[0:THIRD]
            parts[1, dy, PLACE_OF[dx, dz]] = piece[THIRD : 2 * THIRD]
            parts[2, dz, PLACE_OF[dx, dy]] = piece[2 * THIRD :]
    for i in (2, 1, 0):
        low, high = CLASSES[i]
        for d in (2, 1, 3):
            for t in range(3):
                send(
                    parts.at[t, d, low:high], incoming.at[t, d - 1, low:high],
                    rs_send, rs_recv.at[t, i], at(around(t, d, 0)),
                )
        if i == 2:
            for place in range(PLANE - 1, -1, -1):
                for d in (2, 1, 3, 0):
                    if (d, place) != (0, 0):
                        send(
                            w_all.at[0], w_all.at[(4 - d) % 4 * PLANE + BACK_OF[place]],
                            w_send_sem, w_recv_sem, at(around(0, d, place)),
                        )
            due(w_all.at[0:63], w_send_sem)
            every_w = due(w_all.at[0:63], w_recv_sem)
    rings = [
        [due(incoming.at[t, :, low:high], rs_recv.at[t, i]) for t in range(3)]
        for i, (low, high) in enumerate(CLASSES)
    ]
    due(incoming, rs_send)

    every_meta()
    own_ky = jnp.where(row < NY // 2, row, row - NY)
    sub64 = lax.broadcasted_iota(jnp.int32, (NXH, 128), 0)
    own_squares = (sub64 * sub64 + own_ky * own_ky).astype(F32) * turn

    def square_row(step, carry):
        px = step // PLANE
        pp = step % PLANE
        wave = sine_of_turns(meta_all[step, 4:5, :] * own_squares + 0.1 / (2.0 * math.pi))
        ctf_sq[px, :, pl.ds(pl.multiple_of(pp * 128, 128), 128)] = (wave * wave).astype(BF16)
        return carry

    lax.fori_loop(0, 64, square_row, 0)


    for i in (2, 1, 0):
        low, high = CLASSES[i]
        for t in range(3):
            rings[i][t]()
            for place in range(high - 1, low - 1, -1):
                total = parts[t, 0, place].astype(F32)
                for d in range(3):
                    total = total + incoming[t, d, place].astype(F32)
                sums[t, place] = total.astype(BF16)
                if place > 0:
                    send(
                        sums.at[t, place], last.at[t, BACK_OF[place] - 1],
                        fin_send, fin_recv.at[t], at(around(t, 0, place)),
                    )
    finals = [due(last.at[t], fin_recv.at[t]) for t in range(3)]
    due(last, fin_send)

    every_w()

    def weigh(px, total):
        blocks = []
        for pp in range(PLANE):
            block = jnp.zeros((CANDS, 128), F32)
            for k in range(K):
                block = block + jnp.where(
                    sub96 == meta_all[px * PLANE + pp, k : k + 1, :], w_all[px * PLANE + pp, k : k + 1, :], 0.0
                )
            blocks.append(block.astype(BF16))
        return total + nt_dot(jnp.concatenate(blocks, axis=1), ctf_sq[px])

    weight_slices = lax.fori_loop(0, RING, weigh, jnp.zeros((CANDS, NXH), F32))

    def backproject(sums, width):
        flat = jnp.concatenate([sums[g * POSES : (g + 1) * POSES] for g in range(CLS)], axis=1)
        high = flat.astype(BF16).astype(F32)
        stacked = jnp.concatenate(
            [high, flat - high, jnp.zeros((128 - 2 * POSES, CLS * width), F32)], axis=0
        )
        return dot(back[...], stacked.astype(BF16)).astype(BF16)

    result = backproject(weight_slices, NXH)
    for j in range(8):
        w_send[j] = result[j * 32 : (j + 1) * 32]
    w_recv[vol] = w_send[vol]
    for pv in members:
        send(w_send.at[pv], w_recv.at[vol], out_send.at[0], out_recv.at[0], (dom, pv))
    due(w_send.at[0:7], out_send.at[0])
    weight_rows = due(w_recv.at[0:7], out_recv.at[0])

    for arrived in finals:
        arrived()
    own = []
    for t in range(3):
        total = sums[t, 0].astype(F32)
        for j in range(PLANE - 1):
            total = total + last[t, j].astype(F32)
        own.append(total)
    own = jnp.concatenate(own, axis=0)
    result = backproject(own, NX2)
    for j in range(8):
        for g in range(CLS):
            data_send[j, g] = result[j * 32 : (j + 1) * 32, g * 128 : (g + 1) * 128]
    for pv in members:
        send(data_send.at[pv], data_out.at[:, :, own_lanes], out_send.at[1], out_recv.at[1], (dom, pv))
    due(data_send.at[0:7], out_send.at[1])
    due(data_send.at[0:7], out_recv.at[1])
    load(data_send.at[vol], data_out.at[:, :, own_lanes], local_sem.at[2])

    weight_rows()
    for pair_of in range(4):
        even = w_recv[2 * pair_of].astype(F32)
        odd = w_recv[2 * pair_of + 1].astype(F32)
        for g in range(CLS):
            lanes = slice(g * NXH, (g + 1) * NXH)
            sq_held[g, :, pair_of * 128 : (pair_of + 1) * 128] = jnp.concatenate(
                [even[:, lanes], odd[:, lanes]], axis=1
            ).astype(BF16)

    load(sq_held, weight_out, local_sem.at[9])

    for ref, sem in under_way.values():
        pltpu.make_async_copy(ref, ref, sem).wait()


def place(weights, data, squares, weights_out, data_out, weight_out, w_held, d_held, s_held, sems):
    chain = ((weights, w_held, weights_out), (data, d_held, data_out), (squares, s_held, weight_out))
    inward = [pltpu.make_async_copy(src, held, sems.at[0, i]) for i, (src, held, _) in enumerate(chain)]
    outward = [pltpu.make_async_copy(held, dst, sems.at[1, i]) for i, (_, held, dst) in enumerate(chain)]
    for copy in inward:
        copy.start()
    for first, second in zip(inward, outward):
        first.wait()
        second.start()
    for copy in outward:
        copy.wait()


def body(volume, images, defocus, inv_noise, class_idx, pose_idx, slab_offset):
    anywhere = pl.BlockSpec(memory_space=pl.ANY)
    dma = pltpu.SemaphoreType.DMA
    V = pltpu.VMEM
    weights, data_acc, weight_acc = pl.pallas_call(
        kernel,
        out_shape=(
            jax.ShapeDtypeStruct((K, 64), F32),
            jax.ShapeDtypeStruct((CLS, 32, 1024), BF16),
            jax.ShapeDtypeStruct((CLS, 32, 512), BF16),
        ),
        in_specs=[anywhere] * 7,
        out_specs=(anywhere,) * 3,
        scratch_shapes=[
            V((1, 64), F32), V((NY, NX2), F32), V((K, 64), jnp.int32), V((K, 64), jnp.int32),
            V((POSES, NY), jnp.int32),
            V((8, 128, 1024), BF16), V((8, 128, 1024), BF16), V((8, 128, 1024), BF16),
            V((8, 128, 1024), BF16), V((128, 128), F32),
            V((8, CLS, 32, 128), BF16), V((NZ, 128), BF16),
            V((8, 128), F32), V((8, 128), F32), V((RING * PLANE, 8, 128), F32),
            V((3, RING, PLANE, THIRD, 128), BF16),
            V((8, 128), F32), V((8, 128), F32),
            V((RING * PLANE, K, 128), F32), V((RING, NXH, PLANE * 128), BF16),
            V((3, RING, PLANE, THIRD, 128), BF16), V((3, RING - 1, PLANE, THIRD, 128), BF16),
            V((3, PLANE, THIRD, 128), BF16), V((3, PLANE - 1, THIRD, 128), BF16),
            V((8, CLS, 32, 128), BF16), V((8, 32, CLS * NXH), BF16), V((8, 32, CLS * NXH), BF16),
            V((K, 64), F32), V((CLS, 32, 512), BF16),
            dma((10,)), dma((3,)), dma((3,)), dma, dma, dma, dma,
            dma, dma((3, 3)), dma, dma((3,)), dma, dma, dma, dma((3, 3)), dma, dma((3,)),
            dma((2,)), dma((2,)),
        ],
        compiler_params=pltpu.CompilerParams(
            collective_id=0, has_side_effects=True, vmem_limit_bytes=60 * 2**20
        ),
    )(
        volume, images, defocus.reshape(1, 64), inv_noise.reshape(NY, NX2),
        class_idx.T, pose_idx.T, slab_offset,
    )
    weights, data_acc, weight_acc = pl.pallas_call(
        place,
        out_shape=tuple(jax.ShapeDtypeStruct(a.shape, a.dtype) for a in (weights, data_acc, weight_acc)),
        in_specs=[anywhere] * 3,
        out_specs=(anywhere,) * 3,
        scratch_shapes=[V(a.shape, a.dtype) for a in (weights, data_acc, weight_acc)] + [dma((2, 3))],
        compiler_params=pltpu.CompilerParams(vmem_limit_bytes=60 * 2**20),
    )(weights, data_acc, weight_acc)
    return weights.T, data_acc, weight_acc


def solution(mesh):
    return jax.shard_map(
        body,
        mesh=mesh,
        in_specs=(
            P(None, "vol", "dom"),
            P(("dom", "vol"), None),
            P(("dom", "vol")),
            P(),
            P(("dom", "vol"), None),
            P(("dom", "vol"), None),
            P(),
        ),
        out_specs=(P(("dom", "vol"), None), P(None, "vol", "dom"), P(None, "vol", "dom")),
        check_vma=False,
    )
```

```python
import functools
import math

import jax
import jax.numpy as jnp
import numpy as np
from jax import lax
from jax.experimental import pallas as pl
from jax.experimental.pallas import tpu as pltpu
from jax.sharding import PartitionSpec as P

MESH = pl.DeviceIdType.MESH
F32 = jnp.float32
BF16 = jnp.bfloat16

CLS = 4
NZ = 256
NY = 128
NXH = 64
NX2 = 128
POSES = 24
K = 4
CANDS = 96
THIRD = 32
RING = 4
PLANE = 16

PLACES = (
    (0, 0), (0, 1), (0, 3), (1, 0), (3, 0),
    (0, 2), (2, 0), (1, 1), (1, 3), (3, 1), (3, 3),
    (1, 2), (3, 2), (2, 1), (2, 3), (2, 2),
)
PLACE_OF = {step: i for i, step in enumerate(PLACES)}
BACK_OF = [PLACE_OF[(-a) % 4, (-b) % 4] for a, b in PLACES]
CLASSES = ((0, 5), (5, 11), (11, 16))
CLASS_OF = [0] * 5 + [1] * 6 + [2] * 5


def around(axis, turn, place):
    first, second = PLACES[place]
    return ((turn, first, second), (first, turn, second), (first, second, turn))[axis]


def sine_coefficients(terms):
    nodes = 0.5 * np.cos((np.arange(200) + 0.5) * math.pi / 400)
    table = np.stack([nodes ** (2 * k + 1) for k in range(terms)], axis=1)
    return np.linalg.lstsq(table, np.sin(2 * math.pi * nodes), rcond=None)[0].tolist()


SINE = sine_coefficients(5)
ROUNDER = 12582912.0


def sine_of_turns(turns):
    rest = turns - ((turns + ROUNDER) - ROUNDER)
    square = rest * rest
    value = SINE[-1] * square + SINE[-2]
    for coefficient in SINE[-3::-1]:
        value = value * square + coefficient
    return value * rest


def nt_dot(left, right):
    return lax.dot_general(left, right, (((1,), (1,)), ((), ())), preferred_element_type=F32)


def dot(left, right):
    return jnp.dot(left, right, preferred_element_type=F32)


def kernel(
    volume, images, defocus, inv_noise, class_idx, pose_idx, slab_offset,
    weights_out, data_out, weight_out,
    focus_in, noise, cls_in, pose_in, slab_in,
    imgs, signal, scaled, quad, focus,
    volrow, back,
    meta_own, meta_sib, meta_all,
    sl,
    part_own, part_sib,
    w_all, ctf_sq, sq_part, sq_in,
    parts, incoming, sums, last,
    data_send, w_send, w_recv, w_held, sq_held,
    local_sem, sib_send, sib_recv, vol_send, vol_recv, meta_send, meta_recv,
    ag_send, ag_recv, ring_send, ring_recv, w_send_sem, w_recv_sem, rs_send, rs_recv, fin_send, fin_recv,
    out_send, out_recv, sq_send, sq_recv,
):
    dom = lax.axis_index("dom")
    vol = lax.axis_index("vol")
    x = (dom // 8) * 2 + vol % 2
    y = (dom // 2) % 4
    z = vol // 2
    c = dom % 2
    row = dom * 8 + vol

    def device(px, py, pz, pc):
        return ((px // 2) * 8 + py * 2 + pc, pz * 2 + px % 2)

    def near(dx, dy, dz):
        return (x + dx) % 4, (y + dy) % 4, (z + dz) % 4

    def send(src, dst, send_sem, recv_sem, target):
        pltpu.make_async_remote_copy(
            src_ref=src, dst_ref=dst, send_sem=send_sem, recv_sem=recv_sem,
            device_id=target, device_id_type=MESH,
        ).start()

    under_way = {}

    def due(ref, sem):
        name = object()
        under_way[name] = (ref, sem)

        def now():
            del under_way[name]
            pltpu.make_async_copy(ref, ref, sem).wait()

        return now

    def load(src, dst, sem):
        pltpu.make_async_copy(src, dst, sem).start()
        return due(dst, sem)

    sibling = device(x, y, z, 1 - c)

    def at(steps):
        return device(*near(*steps), c)

    barrier = pltpu.get_barrier_semaphore()
    pl.semaphore_signal(barrier, inc=1, device_id=sibling, device_id_type=MESH)
    for k in range(1, 8):
        pl.semaphore_signal(barrier, inc=1, device_id=(dom, (vol + k) % 8), device_id_type=MESH)
        pl.semaphore_signal(barrier, inc=1, device_id=((dom + 2 * k) % 16, vol), device_id_type=MESH)

    def own_images(b):
        return images.at[:, pl.ds(pl.multiple_of((2 * b + c) * 1024, 1024), 1024)]

    def other_images(b):
        return images.at[:, pl.ds(pl.multiple_of((2 * b + 1 - c) * 1024, 1024), 1024)]

    mine = pl.ds(pl.multiple_of(c * 64, 64), 64)
    own_lanes = pl.ds(pl.multiple_of(vol * 128, 128), 128)
    own_volume = load(volume.at[:, :, own_lanes], volrow.at[vol], local_sem.at[1])
    for b in range(8):
        pltpu.make_async_copy(own_images(b), imgs.at[b, mine], local_sem.at[0]).start()
    local_images = due(imgs.at[:, 0:64], local_sem.at[0])
    small = [
        load(class_idx, cls_in, local_sem.at[3]),
        load(pose_idx, pose_in, local_sem.at[4]),
        load(defocus, focus_in, local_sem.at[5]),
        load(slab_offset, slab_in, local_sem.at[6]),
        load(inv_noise, noise, local_sem.at[7]),
    ]
    pl.semaphore_wait(barrier, 15)

    vol_steps = ((2, 1), (1, 1), (3, 1), (2, 0), (1, 0), (3, 0), (0, 1))
    members = [((z + dz) % 4) * 2 + (vol + dx) % 2 for dz, dx in vol_steps]
    for pv in members:
        send(
            volume.at[:, :, pl.ds(pl.multiple_of(pv * 128, 128), 128)], volrow.at[vol],
            vol_send, vol_recv, (dom, pv),
        )
    volume_rows = due(volrow.at[0:7], vol_recv)
    due(volrow.at[0:7], vol_send)
    for b in range(8):
        send(other_images(b), imgs.at[b, mine], sib_send.at[1], sib_recv.at[1], sibling)
    for arrived in small:
        arrived()

    pair = (cls_in[...] * POSES + pose_in[...]).astype(F32)
    meta_own[...] = jnp.concatenate(
        [jnp.concatenate([pair, focus_in[...], jnp.zeros((3, 64), F32)], axis=0), jnp.zeros((8, 64), F32)], axis=1
    )

    send(meta_own, meta_sib, sib_send.at[0], sib_recv.at[0], sibling)
    sibling_meta = due(meta_sib, sib_recv.at[0])
    due(meta_own, sib_send.at[0])
    sibling_images = due(imgs.at[:, 0:64], sib_recv.at[1])
    due(imgs.at[:, 0:64], sib_send.at[1])

    sibling_meta()
    lane8 = lax.broadcasted_iota(jnp.int32, (8, 128), 1)
    first = jnp.where(c == 0, meta_own[...], meta_sib[...])
    second = jnp.where(c == 0, meta_sib[...], meta_own[...])
    meta = jnp.where(lane8 < 64, first, pltpu.roll(second, 64, 1))
    meta_all[0] = meta
    for k in range(1, 8):
        send(meta_all.at[0], meta_all.at[8 - k], meta_send, meta_recv, ((dom + 2 * k) % 16, vol))
    due(meta_all.at[0:7], meta_send)
    dom_meta = due(meta_all.at[0:7], meta_recv)
    columns = jnp.transpose(jnp.concatenate([meta, jnp.zeros((120, 128), F32)], axis=0))
    focus[...] = jnp.broadcast_to(columns[:, 4:5], (128, 128))

    lane_row = lax.broadcasted_iota(jnp.int32, (1, 128), 1) % NXH
    kx_sq = (lane_row * lane_row).astype(F32)
    turn = 6.0 / (2.0 * math.pi * (NY // 2) ** 2)

    def prepare(step, carry):
        px, py, pz = near(step // 16, (step // 4) % 4, step % 4)
        b = (px // 2) * 4 + py
        v = pz * 2 + px % 2
        r = (2 * b + c) * 8 + v
        ky = jnp.where(r < NY // 2, r, r - NY)
        squares = (kx_sq + (ky * ky).astype(F32)) * turn
        lanes = pl.ds(pl.multiple_of(v * 128, 128), 128)
        group = step // 8
        spot = pl.ds(pl.multiple_of((step % 8) * 128, 128), 128)
        contrast = -sine_of_turns(focus[...] * squares + 0.1 / (2.0 * math.pi))
        seen = contrast * imgs[b, :, lanes].astype(F32)
        level = noise[pl.ds(r, 1), :]
        signal[group, :, spot] = seen.astype(BF16)
        scaled[group, :, spot] = (seen * level).astype(BF16)
        quad[group, :, spot] = (contrast * contrast * (-0.5 * level)).astype(BF16)
        return carry

    local_images()
    sibling_images()
    lax.fori_loop(0, 8, prepare, 0)

    lane24 = lax.broadcasted_iota(jnp.int32, (POSES, 128), 1)
    offset = jnp.sum(jnp.where(lane24 == row, slab_in[...].astype(F32), 0.0), axis=1, keepdims=True)
    offset = offset.astype(jnp.int32)
    whole = lax.shift_right_arithmetic(offset, 4)
    lower = lax.bitwise_and(whole, NZ - 1)
    upper = lax.bitwise_and(whole + 1, NZ - 1)
    fraction = lax.bitwise_and(offset, 15).astype(F32) * (1.0 / 16.0)
    slab = lax.broadcasted_iota(jnp.int32, (POSES, NZ), 1)
    interp = jnp.where(slab == lower, 1.0 - fraction, 0.0) + jnp.where(slab == upper, fraction, 0.0)
    padded = jnp.concatenate([interp, interp, jnp.zeros((128 - 2 * POSES, NZ), F32)], axis=0)
    back[...] = jnp.transpose(padded).astype(BF16)

    own_volume()
    volume_rows()
    narrow = interp.astype(BF16)
    rows = [
        dot(narrow, jnp.concatenate([volrow[j, g] for j in range(8)], axis=0)) for g in range(CLS)
    ]
    slices = jnp.concatenate(rows, axis=0).astype(BF16)
    for t in range(3):
        sl[t, 0, 0] = slices[t * THIRD : (t + 1) * THIRD]
    for place in (*range(1, 5), *range(15, 4, -1)):
        for t in range(3):
            send(
                sl.at[t, 0, 0], sl.at[t, 0, BACK_OF[place]],
                ag_send, ag_recv.at[t, CLASS_OF[place]], at(around(t, 0, place)),
            )
    planes = [
        [due(sl.at[t, 0, max(low, 1) : high], ag_recv.at[t, i]) for t in range(3)]
        for i, (low, high) in enumerate(CLASSES)
    ]
    due(sl.at[:, 0, 0:15], ag_send)
    lax.fori_loop(8, 24, prepare, 0)

    for i, (low, high) in enumerate(CLASSES):
        for t in range(3):
            planes[i][t]()
            for d in (2, 1, 3):
                send(
                    sl.at[t, 0, low:high], sl.at[t, 4 - d, low:high],
                    ring_send, ring_recv.at[t], at(around(t, d, 0)),
                )
    rest = [due(sl.at[t, 1:4], ring_recv.at[t]) for t in range(3)]
    due(sl.at[:, 1:4], ring_send)
    lax.fori_loop(24, 64, prepare, 0)

    for arrived in rest:
        arrived()

    scores = jnp.zeros((CANDS, 128), F32)
    for group in range(8):
        pieces = []
        for step in range(8 * group, 8 * group + 8):
            dx, dy, dz = step // 16, (step // 4) % 4, step % 4
            pieces.append(
                jnp.concatenate(
                    [
                        sl[0, dx, PLACE_OF[dy, dz]],
                        sl[1, dy, PLACE_OF[dx, dz]],
                        sl[2, dz, PLACE_OF[dx, dy]],
                    ],
                    axis=0,
                )
            )
        band = jnp.concatenate(pieces, axis=1)
        wide_band = band.astype(F32)
        band_sq = (wide_band * wide_band).astype(BF16)
        scores = scores + nt_dot(band, scaled[group]) + nt_dot(band_sq, quad[group])
    sub96 = lax.broadcasted_iota(jnp.int32, (CANDS, 128), 0).astype(F32)
    picked = [
        jnp.sum(jnp.where(sub96 == meta[k : k + 1], scores, 0.0), axis=0, keepdims=True) for k in range(K)
    ]
    part_own[...] = jnp.concatenate(picked + [jnp.zeros((4, 128), F32)], axis=0)
    send(part_own, part_sib, sib_send.at[2], sib_recv.at[2], sibling)
    due(part_own, sib_send.at[2])
    sibling_part = due(part_sib, sib_recv.at[2])
    sibling_part()
    both = (part_own[...] + part_sib[...])[0:K]
    best = jnp.max(both, axis=0, keepdims=True)
    grown = jnp.exp(both - best)
    weights = grown / jnp.sum(grown, axis=0, keepdims=True)
    w_all[0] = weights
    for k in range(1, 8):
        send(w_all.at[0], w_all.at[8 - k], w_send_sem, w_recv_sem, ((dom + 2 * k) % 16, vol))
    due(w_all.at[0:7], w_send_sem)
    dom_w = due(w_all.at[0:7], w_recv_sem)
    w_held[...] = jnp.where(c == 0, weights, pltpu.roll(weights, 64, 1))[:, 0:64]
    load(w_held, weights_out, local_sem.at[8])

    spread = jnp.zeros((CANDS, 128), F32)
    for k in range(K):
        spread = spread + jnp.where(sub96 == meta[k : k + 1], weights[k : k + 1], 0.0)
    spread = spread.astype(BF16)

    for group in range(8):
        band = dot(spread, signal[group]).astype(BF16)
        for i in range(8):
            step = 8 * group + i
            dx, dy, dz = step // 16, (step // 4) % 4, step % 4
            piece = band[:, i * 128 : (i + 1) * 128]
            parts[0, dx, PLACE_OF[dy, dz]] = piece[0:THIRD]
            parts[1, dy, PLACE_OF[dx, dz]] = piece[THIRD : 2 * THIRD]
            parts[2, dz, PLACE_OF[dx, dy]] = piece[2 * THIRD :]
    for i in (2, 1, 0):
        low, high = CLASSES[i]
        for d in (2, 1, 3):
            for t in range(3):
                send(
                    parts.at[t, d, low:high], incoming.at[t, d - 1, low:high],
                    rs_send, rs_recv.at[t, i], at(around(t, d, 0)),
                )
    rings = [
        [due(incoming.at[t, :, low:high], rs_recv.at[t, i]) for t in range(3)]
        for i, (low, high) in enumerate(CLASSES)
    ]
    due(incoming, rs_send)

    dom_meta()
    sub64 = lax.broadcasted_iota(jnp.int32, (NXH, 128), 0)

    def square_row(step, carry):
        band_row = step // 8
        k = step % 8
        r = dom * 8 + band_row
        ky = jnp.where(r < NY // 2, r, r - NY)
        squares = (sub64 * sub64 + ky * ky).astype(F32) * turn
        wave = sine_of_turns(meta_all[k, 4:5, :] * squares + 0.1 / (2.0 * math.pi))
        ctf_sq[band_row, :, pl.ds(pl.multiple_of(k * 128, 128), 128)] = (wave * wave).astype(BF16)
        return carry

    lax.fori_loop(0, 64, square_row, 0)

    dom_w()
    blocks = []
    for k in range(8):
        block = jnp.zeros((CANDS, 128), F32)
        for j in range(K):
            block = block + jnp.where(sub96 == meta_all[k, j : j + 1, :], w_all[k, j : j + 1, :], 0.0)
        blocks.append(block.astype(BF16))
    blocks = jnp.concatenate(blocks, axis=1)
    for band_row in range(8):
        part = nt_dot(blocks, ctf_sq[band_row])
        sq_part[band_row] = jnp.concatenate([part[0:48], part[48:96]], axis=1).astype(BF16)
    sq_in[vol] = sq_part[vol]
    for pv in members:
        send(sq_part.at[pv], sq_in.at[vol], sq_send, sq_recv, (dom, pv))
    due(sq_part.at[0:7], sq_send)
    vol_parts = due(sq_in.at[0:7], sq_recv)

    for i in (2, 1, 0):
        low, high = CLASSES[i]
        for t in range(3):
            rings[i][t]()
            for place in range(high - 1, low - 1, -1):
                total = parts[t, 0, place].astype(F32)
                for d in range(3):
                    total = total + incoming[t, d, place].astype(F32)
                sums[t, place] = total.astype(BF16)
                if place > 0:
                    send(
                        sums.at[t, place], last.at[t, BACK_OF[place] - 1],
                        fin_send, fin_recv.at[t], at(around(t, 0, place)),
                    )
    finals = [due(last.at[t], fin_recv.at[t]) for t in range(3)]
    due(last, fin_send)

    vol_parts()
    folded = sq_in[0].astype(F32)
    for j in range(1, 8):
        folded = folded + sq_in[j].astype(F32)
    weight_slices = jnp.concatenate([folded[:, 0:NXH], folded[:, NXH:]], axis=0)

    def backproject(classes):
        flat = jnp.concatenate(classes, axis=1)
        high = flat.astype(BF16).astype(F32)
        stacked = jnp.concatenate(
            [high, flat - high, jnp.zeros((128 - 2 * POSES, flat.shape[1]), F32)], axis=0
        )
        return dot(back[...], stacked.astype(BF16)).astype(BF16)

    result = backproject([weight_slices[g * POSES : (g + 1) * POSES] for g in range(CLS)])
    for j in range(8):
        w_send[j] = result[j * 32 : (j + 1) * 32]
    w_recv[vol] = w_send[vol]
    for pv in members:
        send(w_send.at[pv], w_recv.at[vol], out_send.at[0], out_recv.at[0], (dom, pv))
    due(w_send.at[0:7], out_send.at[0])
    weight_rows = due(w_recv.at[0:7], out_recv.at[0])

    own = []
    for g in range(CLS):
        while len(own) * THIRD < (g + 1) * POSES:
            t = len(own)
            finals[t]()
            total = sums[t, 0].astype(F32)
            for j in range(PLANE - 1):
                total = total + last[t, j].astype(F32)
            own.append(total)
        joined = jnp.concatenate(own, axis=0)
        result = backproject([joined[g * POSES : (g + 1) * POSES]])
        for j in range(8):
            data_send[j, g] = result[j * 32 : (j + 1) * 32]
        for pv in members:
            send(data_send.at[pv, g], data_out.at[g, :, own_lanes], out_send.at[1], out_recv.at[1], (dom, pv))
    due(data_send.at[0:7], out_send.at[1])
    due(data_send.at[0:7], out_recv.at[1])
    load(data_send.at[vol], data_out.at[:, :, own_lanes], local_sem.at[2])

    weight_rows()
    for pair_of in range(4):
        even = w_recv[2 * pair_of].astype(F32)
        odd = w_recv[2 * pair_of + 1].astype(F32)
        for g in range(CLS):
            lanes = slice(g * NXH, (g + 1) * NXH)
            sq_held[g, :, pair_of * 128 : (pair_of + 1) * 128] = jnp.concatenate(
                [even[:, lanes], odd[:, lanes]], axis=1
            ).astype(BF16)

    load(sq_held, weight_out, local_sem.at[9])

    for ref, sem in under_way.values():
        pltpu.make_async_copy(ref, ref, sem).wait()


def place(weights, data, squares, weights_out, data_out, weight_out, w_held, d_held, s_held, sems):
    chain = ((weights, w_held, weights_out), (data, d_held, data_out), (squares, s_held, weight_out))
    inward = [pltpu.make_async_copy(src, held, sems.at[0, i]) for i, (src, held, _) in enumerate(chain)]
    outward = [pltpu.make_async_copy(held, dst, sems.at[1, i]) for i, (_, held, dst) in enumerate(chain)]
    for copy in inward:
        copy.start()
    for first, second in zip(inward, outward):
        first.wait()
        second.start()
    for copy in outward:
        copy.wait()


def body(volume, images, defocus, inv_noise, class_idx, pose_idx, slab_offset):
    anywhere = pl.BlockSpec(memory_space=pl.ANY)
    dma = pltpu.SemaphoreType.DMA
    V = pltpu.VMEM
    weights, data_acc, weight_acc = pl.pallas_call(
        kernel,
        out_shape=(
            jax.ShapeDtypeStruct((K, 64), F32),
            jax.ShapeDtypeStruct((CLS, 32, 1024), BF16),
            jax.ShapeDtypeStruct((CLS, 32, 512), BF16),
        ),
        in_specs=[anywhere] * 7,
        out_specs=(anywhere,) * 3,
        scratch_shapes=[
            V((1, 64), F32), V((NY, NX2), F32), V((K, 64), jnp.int32), V((K, 64), jnp.int32),
            V((POSES, NY), jnp.int32),
            V((8, 128, 1024), BF16), V((8, 128, 1024), BF16), V((8, 128, 1024), BF16),
            V((8, 128, 1024), BF16), V((128, 128), F32),
            V((8, CLS, 32, 128), BF16), V((NZ, 128), BF16),
            V((8, 128), F32), V((8, 128), F32), V((8, 8, 128), F32),
            V((3, RING, PLANE, THIRD, 128), BF16),
            V((8, 128), F32), V((8, 128), F32),
            V((8, K, 128), F32), V((8, NXH, 1024), BF16),
            V((8, 48, 128), BF16), V((8, 48, 128), BF16),
            V((3, RING, PLANE, THIRD, 128), BF16), V((3, RING - 1, PLANE, THIRD, 128), BF16),
            V((3, PLANE, THIRD, 128), BF16), V((3, PLANE - 1, THIRD, 128), BF16),
            V((8, CLS, 32, 128), BF16), V((8, 32, CLS * NXH), BF16), V((8, 32, CLS * NXH), BF16),
            V((K, 64), F32), V((CLS, 32, 512), BF16),
            dma((10,)), dma((3,)), dma((3,)), dma, dma, dma, dma,
            dma, dma((3, 3)), dma, dma((3,)), dma, dma, dma, dma((3, 3)), dma, dma((3,)),
            dma((2,)), dma((2,)), dma, dma,
        ],
        compiler_params=pltpu.CompilerParams(
            collective_id=0, has_side_effects=True, vmem_limit_bytes=60 * 2**20
        ),
    )(
        volume, images, defocus.reshape(1, 64), inv_noise.reshape(NY, NX2),
        class_idx.T, pose_idx.T, slab_offset,
    )
    weights, data_acc, weight_acc = pl.pallas_call(
        place,
        out_shape=tuple(jax.ShapeDtypeStruct(a.shape, a.dtype) for a in (weights, data_acc, weight_acc)),
        in_specs=[anywhere] * 3,
        out_specs=(anywhere,) * 3,
        scratch_shapes=[V(a.shape, a.dtype) for a in (weights, data_acc, weight_acc)] + [dma((2, 3))],
        compiler_params=pltpu.CompilerParams(vmem_limit_bytes=60 * 2**20),
    )(weights, data_acc, weight_acc)
    return weights.T, data_acc, weight_acc


def solution(mesh):
    return jax.shard_map(
        body,
        mesh=mesh,
        in_specs=(
            P(None, "vol", "dom"),
            P(("dom", "vol"), None),
            P(("dom", "vol")),
            P(),
            P(("dom", "vol"), None),
            P(("dom", "vol"), None),
            P(),
        ),
        out_specs=(P(("dom", "vol"), None), P(None, "vol", "dom"), P(None, "vol", "dom")),
        check_vma=False,
    )
```

```python
import functools
import math

import jax
import jax.numpy as jnp
import numpy as np
from jax import lax
from jax.experimental import pallas as pl
from jax.experimental.pallas import tpu as pltpu
from jax.sharding import PartitionSpec as P

MESH = pl.DeviceIdType.MESH
F32 = jnp.float32
BF16 = jnp.bfloat16

CLS = 4
NZ = 256
NY = 128
NXH = 64
NX2 = 128
POSES = 24
K = 4
CANDS = 96
THIRD = 32
RING = 4
PLANE = 16

PLACES = (
    (0, 0), (0, 1), (0, 3), (1, 0), (3, 0),
    (0, 2), (2, 0), (1, 1), (1, 3), (3, 1), (3, 3),
    (1, 2), (3, 2), (2, 1), (2, 3), (2, 2),
)
PLACE_OF = {step: i for i, step in enumerate(PLACES)}
BACK_OF = [PLACE_OF[(-a) % 4, (-b) % 4] for a, b in PLACES]
CLASSES = ((0, 5), (5, 11), (11, 16))
RS_CLASSES = ((0, 11), (11, 16))
CLASS_OF = [0] * 5 + [1] * 6 + [2] * 5


def around(axis, turn, place):
    first, second = PLACES[place]
    return ((turn, first, second), (first, turn, second), (first, second, turn))[axis]


def sine_coefficients(terms):
    nodes = 0.5 * np.cos((np.arange(200) + 0.5) * math.pi / 400)
    table = np.stack([nodes ** (2 * k + 1) for k in range(terms)], axis=1)
    return np.linalg.lstsq(table, np.sin(2 * math.pi * nodes), rcond=None)[0].tolist()


SINE = sine_coefficients(5)
ROUNDER = 12582912.0


def sine_of_turns(turns):
    rest = turns - ((turns + ROUNDER) - ROUNDER)
    square = rest * rest
    value = SINE[-1] * square + SINE[-2]
    for coefficient in SINE[-3::-1]:
        value = value * square + coefficient
    return value * rest


def nt_dot(left, right):
    return lax.dot_general(left, right, (((1,), (1,)), ((), ())), preferred_element_type=F32)


def dot(left, right):
    return jnp.dot(left, right, preferred_element_type=F32)


def kernel(
    volume, images, defocus, inv_noise, class_idx, pose_idx, slab_offset,
    weights_out, data_out, weight_out,
    focus_in, noise, cls_in, pose_in, slab_in,
    imgs, signal, scaled, quad, focus,
    volrow, back,
    meta_own, meta_sib, meta_all,
    sl,
    part_own, part_sib,
    w_all, ctf_sq, sq_part, sq_in,
    parts, incoming, sums, last,
    data_send, w_send, w_recv, w_held, sq_held,
    local_sem, sib_send, sib_recv, vol_send, vol_recv, meta_send, meta_recv,
    ag_send, ag_recv, ring_send, ring_recv, w_send_sem, w_recv_sem, rs_send, rs_recv, fin_send, fin_recv,
    out_send, out_recv, sq_send, sq_recv,
):
    dom = lax.axis_index("dom")
    vol = lax.axis_index("vol")
    x = (dom // 8) * 2 + vol % 2
    y = (dom // 2) % 4
    z = vol // 2
    c = dom % 2
    row = dom * 8 + vol

    def device(px, py, pz, pc):
        return ((px // 2) * 8 + py * 2 + pc, pz * 2 + px % 2)

    def near(dx, dy, dz):
        return (x + dx) % 4, (y + dy) % 4, (z + dz) % 4

    def send(src, dst, send_sem, recv_sem, target):
        pltpu.make_async_remote_copy(
            src_ref=src, dst_ref=dst, send_sem=send_sem, recv_sem=recv_sem,
            device_id=target, device_id_type=MESH,
        ).start()

    under_way = {}

    def due(ref, sem):
        name = object()
        under_way[name] = (ref, sem)

        def now():
            del under_way[name]
            pltpu.make_async_copy(ref, ref, sem).wait()

        return now

    def load(src, dst, sem):
        pltpu.make_async_copy(src, dst, sem).start()
        return due(dst, sem)

    sibling = device(x, y, z, 1 - c)

    def at(steps):
        return device(*near(*steps), c)

    barrier = pltpu.get_barrier_semaphore()
    pl.semaphore_signal(barrier, inc=1, device_id=sibling, device_id_type=MESH)
    for k in range(1, 8):
        pl.semaphore_signal(barrier, inc=1, device_id=(dom, (vol + k) % 8), device_id_type=MESH)
        pl.semaphore_signal(barrier, inc=1, device_id=((dom + 2 * k) % 16, vol), device_id_type=MESH)

    def own_images(b):
        return images.at[:, pl.ds(pl.multiple_of((2 * b + c) * 1024, 1024), 1024)]

    def other_images(b):
        return images.at[:, pl.ds(pl.multiple_of((2 * b + 1 - c) * 1024, 1024), 1024)]

    mine = pl.ds(pl.multiple_of(c * 64, 64), 64)
    own_lanes = pl.ds(pl.multiple_of(vol * 128, 128), 128)
    own_volume = load(volume.at[:, :, own_lanes], volrow.at[vol], local_sem.at[1])
    for b in range(8):
        pltpu.make_async_copy(own_images(b), imgs.at[b, mine], local_sem.at[0]).start()
    local_images = due(imgs.at[:, 0:64], local_sem.at[0])
    small = [
        load(class_idx, cls_in, local_sem.at[3]),
        load(pose_idx, pose_in, local_sem.at[4]),
        load(defocus, focus_in, local_sem.at[5]),
        load(slab_offset, slab_in, local_sem.at[6]),
        load(inv_noise, noise, local_sem.at[7]),
    ]
    pl.semaphore_wait(barrier, 15)

    vol_steps = ((2, 1), (1, 1), (3, 1), (2, 0), (1, 0), (3, 0), (0, 1))
    members = [((z + dz) % 4) * 2 + (vol + dx) % 2 for dz, dx in vol_steps]
    for pv in members:
        send(
            volume.at[:, :, pl.ds(pl.multiple_of(pv * 128, 128), 128)], volrow.at[vol],
            vol_send, vol_recv, (dom, pv),
        )
    volume_rows = due(volrow.at[0:7], vol_recv)
    due(volrow.at[0:7], vol_send)
    for b in range(8):
        send(other_images(b), imgs.at[b, mine], sib_send.at[1], sib_recv.at[1], sibling)
    for arrived in small:
        arrived()

    pair = (cls_in[...] * POSES + pose_in[...]).astype(F32)
    meta_own[...] = jnp.concatenate(
        [jnp.concatenate([pair, focus_in[...], jnp.zeros((3, 64), F32)], axis=0), jnp.zeros((8, 64), F32)], axis=1
    )

    send(meta_own, meta_sib, sib_send.at[0], sib_recv.at[0], sibling)
    sibling_meta = due(meta_sib, sib_recv.at[0])
    due(meta_own, sib_send.at[0])
    sibling_images = due(imgs.at[:, 0:64], sib_recv.at[1])
    due(imgs.at[:, 0:64], sib_send.at[1])

    sibling_meta()
    lane8 = lax.broadcasted_iota(jnp.int32, (8, 128), 1)
    first = jnp.where(c == 0, meta_own[...], meta_sib[...])
    second = jnp.where(c == 0, meta_sib[...], meta_own[...])
    meta = jnp.where(lane8 < 64, first, pltpu.roll(second, 64, 1))
    meta_all[0] = meta
    for k in range(1, 8):
        send(meta_all.at[0], meta_all.at[8 - k], meta_send, meta_recv, ((dom + 2 * k) % 16, vol))
    due(meta_all.at[0:7], meta_send)
    dom_meta = due(meta_all.at[0:7], meta_recv)
    columns = jnp.transpose(jnp.concatenate([meta, jnp.zeros((120, 128), F32)], axis=0))
    focus[...] = jnp.broadcast_to(columns[:, 4:5], (128, 128))

    lane_row = lax.broadcasted_iota(jnp.int32, (1, 128), 1) % NXH
    kx_sq = (lane_row * lane_row).astype(F32)
    turn = 6.0 / (2.0 * math.pi * (NY // 2) ** 2)

    def prepare(step, carry):
        px, py, pz = near(step // 16, (step // 4) % 4, step % 4)
        b = (px // 2) * 4 + py
        v = pz * 2 + px % 2
        r = (2 * b + c) * 8 + v
        ky = jnp.where(r < NY // 2, r, r - NY)
        squares = (kx_sq + (ky * ky).astype(F32)) * turn
        lanes = pl.ds(pl.multiple_of(v * 128, 128), 128)
        group = step // 8
        spot = pl.ds(pl.multiple_of((step % 8) * 128, 128), 128)
        contrast = -sine_of_turns(focus[...] * squares + 0.1 / (2.0 * math.pi))
        seen = contrast * imgs[b, :, lanes].astype(F32)
        level = noise[pl.ds(r, 1), :]
        signal[group, :, spot] = seen.astype(BF16)
        scaled[group, :, spot] = (seen * level).astype(BF16)
        quad[group, :, spot] = (contrast * contrast * (-0.5 * level)).astype(BF16)
        return carry

    local_images()
    sibling_images()
    lax.fori_loop(0, 8, prepare, 0)

    lane24 = lax.broadcasted_iota(jnp.int32, (POSES, 128), 1)
    offset = jnp.sum(jnp.where(lane24 == row, slab_in[...].astype(F32), 0.0), axis=1, keepdims=True)
    offset = offset.astype(jnp.int32)
    whole = lax.shift_right_arithmetic(offset, 4)
    lower = lax.bitwise_and(whole, NZ - 1)
    upper = lax.bitwise_and(whole + 1, NZ - 1)
    fraction = lax.bitwise_and(offset, 15).astype(F32) * (1.0 / 16.0)
    slab = lax.broadcasted_iota(jnp.int32, (POSES, NZ), 1)
    interp = jnp.where(slab == lower, 1.0 - fraction, 0.0) + jnp.where(slab == upper, fraction, 0.0)
    padded = jnp.concatenate([interp, interp, jnp.zeros((128 - 2 * POSES, NZ), F32)], axis=0)
    back[...] = jnp.transpose(padded).astype(BF16)

    own_volume()
    volume_rows()
    narrow = interp.astype(BF16)
    rows = [
        dot(narrow, jnp.concatenate([volrow[j, g] for j in range(8)], axis=0)) for g in range(CLS)
    ]
    slices = jnp.concatenate(rows, axis=0).astype(BF16)
    for t in range(3):
        sl[t, 0, 0] = slices[t * THIRD : (t + 1) * THIRD]
    for place in (*range(1, 5), *range(15, 4, -1)):
        for t in range(3):
            send(
                sl.at[t, 0, 0], sl.at[t, 0, BACK_OF[place]],
                ag_send, ag_recv.at[t, CLASS_OF[place]], at(around(t, 0, place)),
            )
    planes = [
        [due(sl.at[t, 0, max(low, 1) : high], ag_recv.at[t, i]) for t in range(3)]
        for i, (low, high) in enumerate(CLASSES)
    ]
    due(sl.at[:, 0, 0:15], ag_send)
    lax.fori_loop(8, 24, prepare, 0)

    for i, (low, high) in enumerate(CLASSES):
        for t in range(3):
            planes[i][t]()
            for d in (2, 1, 3):
                send(
                    sl.at[t, 0, low:high], sl.at[t, 4 - d, low:high],
                    ring_send, ring_recv.at[t], at(around(t, d, 0)),
                )
    rest = [due(sl.at[t, 1:4], ring_recv.at[t]) for t in range(3)]
    due(sl.at[:, 1:4], ring_send)
    lax.fori_loop(24, 64, prepare, 0)

    for arrived in rest:
        arrived()

    scores = jnp.zeros((CANDS, 128), F32)
    for group in range(8):
        pieces = []
        for step in range(8 * group, 8 * group + 8):
            dx, dy, dz = step // 16, (step // 4) % 4, step % 4
            pieces.append(
                jnp.concatenate(
                    [
                        sl[0, dx, PLACE_OF[dy, dz]],
                        sl[1, dy, PLACE_OF[dx, dz]],
                        sl[2, dz, PLACE_OF[dx, dy]],
                    ],
                    axis=0,
                )
            )
        band = jnp.concatenate(pieces, axis=1)
        wide_band = band.astype(F32)
        band_sq = (wide_band * wide_band).astype(BF16)
        scores = scores + nt_dot(band, scaled[group]) + nt_dot(band_sq, quad[group])
    sub96 = lax.broadcasted_iota(jnp.int32, (CANDS, 128), 0).astype(F32)
    picked = [
        jnp.sum(jnp.where(sub96 == meta[k : k + 1], scores, 0.0), axis=0, keepdims=True) for k in range(K)
    ]
    part_own[...] = jnp.concatenate(picked + [jnp.zeros((4, 128), F32)], axis=0)
    send(part_own, part_sib, sib_send.at[2], sib_recv.at[2], sibling)
    due(part_own, sib_send.at[2])
    sibling_part = due(part_sib, sib_recv.at[2])
    sibling_part()
    both = (part_own[...] + part_sib[...])[0:K]
    best = jnp.max(both, axis=0, keepdims=True)
    grown = jnp.exp(both - best)
    weights = grown / jnp.sum(grown, axis=0, keepdims=True)
    w_all[0] = weights
    for k in range(1, 8):
        send(w_all.at[0], w_all.at[8 - k], w_send_sem, w_recv_sem, ((dom + 2 * k) % 16, vol))
    due(w_all.at[0:7], w_send_sem)
    dom_w = due(w_all.at[0:7], w_recv_sem)
    w_held[...] = jnp.where(c == 0, weights, pltpu.roll(weights, 64, 1))[:, 0:64]
    load(w_held, weights_out, local_sem.at[8])

    spread = jnp.zeros((CANDS, 128), F32)
    for k in range(K):
        spread = spread + jnp.where(sub96 == meta[k : k + 1], weights[k : k + 1], 0.0)
    spread = spread.astype(BF16)

    for group in range(8):
        band = dot(spread, signal[group]).astype(BF16)
        for i in range(8):
            step = 8 * group + i
            dx, dy, dz = step // 16, (step // 4) % 4, step % 4
            piece = band[:, i * 128 : (i + 1) * 128]
            parts[0, dx, PLACE_OF[dy, dz]] = piece[0:THIRD]
            parts[1, dy, PLACE_OF[dx, dz]] = piece[THIRD : 2 * THIRD]
            parts[2, dz, PLACE_OF[dx, dy]] = piece[2 * THIRD :]
    for i in (1, 0):
        low, high = RS_CLASSES[i]
        for d in (2, 1, 3):
            for t in range(3):
                send(
                    parts.at[t, d, low:high], incoming.at[t, d - 1, low:high],
                    rs_send, rs_recv.at[t, i], at(around(t, d, 0)),
                )
    rings = [
        [due(incoming.at[t, :, low:high], rs_recv.at[t, i]) for t in range(3)]
        for i, (low, high) in enumerate(RS_CLASSES)
    ]
    due(incoming, rs_send)

    dom_meta()
    sub64 = lax.broadcasted_iota(jnp.int32, (NXH, 128), 0)

    def square_row(step, carry):
        band_row = step // 8
        k = step % 8
        r = dom * 8 + band_row
        ky = jnp.where(r < NY // 2, r, r - NY)
        squares = (sub64 * sub64 + ky * ky).astype(F32) * turn
        wave = sine_of_turns(meta_all[k, 4:5, :] * squares + 0.1 / (2.0 * math.pi))
        ctf_sq[band_row, :, pl.ds(pl.multiple_of(k * 128, 128), 128)] = (wave * wave).astype(BF16)
        return carry

    lax.fori_loop(0, 64, square_row, 0)

    dom_w()
    blocks = []
    for k in range(8):
        block = jnp.zeros((CANDS, 128), F32)
        for j in range(K):
            block = block + jnp.where(sub96 == meta_all[k, j : j + 1, :], w_all[k, j : j + 1, :], 0.0)
        blocks.append(block.astype(BF16))
    blocks = jnp.concatenate(blocks, axis=1)
    for band_row in range(8):
        part = nt_dot(blocks, ctf_sq[band_row])
        sq_part[band_row] = jnp.concatenate([part[0:48], part[48:96]], axis=1).astype(BF16)
    sq_in[vol] = sq_part[vol]
    for pv in members:
        send(sq_part.at[pv], sq_in.at[vol], sq_send, sq_recv, (dom, pv))
    due(sq_part.at[0:7], sq_send)
    vol_parts = due(sq_in.at[0:7], sq_recv)

    for i in (1, 0):
        low, high = RS_CLASSES[i]
        for t in range(3):
            rings[i][t]()
            for place in range(high - 1, low - 1, -1):
                total = parts[t, 0, place].astype(F32)
                for d in range(3):
                    total = total + incoming[t, d, place].astype(F32)
                sums[t, place] = total.astype(BF16)
                if place > 0:
                    send(
                        sums.at[t, place], last.at[t, BACK_OF[place] - 1],
                        fin_send, fin_recv.at[t], at(around(t, 0, place)),
                    )
    finals = [due(last.at[t], fin_recv.at[t]) for t in range(3)]
    due(last, fin_send)

    vol_parts()
    folded = sq_in[0].astype(F32)
    for j in range(1, 8):
        folded = folded + sq_in[j].astype(F32)
    weight_slices = jnp.concatenate([folded[:, 0:NXH], folded[:, NXH:]], axis=0)

    def backproject(classes):
        flat = jnp.concatenate(classes, axis=1)
        high = flat.astype(BF16).astype(F32)
        stacked = jnp.concatenate(
            [high, flat - high, jnp.zeros((128 - 2 * POSES, flat.shape[1]), F32)], axis=0
        )
        return dot(back[...], stacked.astype(BF16)).astype(BF16)

    result = backproject([weight_slices[g * POSES : (g + 1) * POSES] for g in range(CLS)])
    for j in range(8):
        w_send[j] = result[j * 32 : (j + 1) * 32]
    w_recv[vol] = w_send[vol]
    for pv in members:
        send(w_send.at[pv], w_recv.at[vol], out_send.at[0], out_recv.at[0], (dom, pv))
    due(w_send.at[0:7], out_send.at[0])
    weight_rows = due(w_recv.at[0:7], out_recv.at[0])

    own = []
    for g in range(CLS):
        while len(own) * THIRD < (g + 1) * POSES:
            t = len(own)
            finals[t]()
            total = sums[t, 0].astype(F32)
            for j in range(PLANE - 1):
                total = total + last[t, j].astype(F32)
            own.append(total)
        joined = jnp.concatenate(own, axis=0)
        result = backproject([joined[g * POSES : (g + 1) * POSES]])
        for j in range(8):
            data_send[j, g] = result[j * 32 : (j + 1) * 32]
        for pv in members:
            send(data_send.at[pv, g], data_out.at[g, :, own_lanes], out_send.at[1], out_recv.at[1], (dom, pv))
    due(data_send.at[0:7], out_send.at[1])
    due(data_send.at[0:7], out_recv.at[1])
    load(data_send.at[vol], data_out.at[:, :, own_lanes], local_sem.at[2])

    weight_rows()
    for pair_of in range(4):
        even = w_recv[2 * pair_of].astype(F32)
        odd = w_recv[2 * pair_of + 1].astype(F32)
        for g in range(CLS):
            lanes = slice(g * NXH, (g + 1) * NXH)
            sq_held[g, :, pair_of * 128 : (pair_of + 1) * 128] = jnp.concatenate(
                [even[:, lanes], odd[:, lanes]], axis=1
            ).astype(BF16)

    load(sq_held, weight_out, local_sem.at[9])

    for ref, sem in under_way.values():
        pltpu.make_async_copy(ref, ref, sem).wait()


def place(weights, data, squares, weights_out, data_out, weight_out, w_held, d_held, s_held, sems):
    chain = ((weights, w_held, weights_out), (data, d_held, data_out), (squares, s_held, weight_out))
    inward = [pltpu.make_async_copy(src, held, sems.at[0, i]) for i, (src, held, _) in enumerate(chain)]
    outward = [pltpu.make_async_copy(held, dst, sems.at[1, i]) for i, (_, held, dst) in enumerate(chain)]
    for copy in inward:
        copy.start()
    for first, second in zip(inward, outward):
        first.wait()
        second.start()
    for copy in outward:
        copy.wait()


def body(volume, images, defocus, inv_noise, class_idx, pose_idx, slab_offset):
    anywhere = pl.BlockSpec(memory_space=pl.ANY)
    dma = pltpu.SemaphoreType.DMA
    V = pltpu.VMEM
    weights, data_acc, weight_acc = pl.pallas_call(
        kernel,
        out_shape=(
            jax.ShapeDtypeStruct((K, 64), F32),
            jax.ShapeDtypeStruct((CLS, 32, 1024), BF16),
            jax.ShapeDtypeStruct((CLS, 32, 512), BF16),
        ),
        in_specs=[anywhere] * 7,
        out_specs=(anywhere,) * 3,
        scratch_shapes=[
            V((1, 64), F32), V((NY, NX2), F32), V((K, 64), jnp.int32), V((K, 64), jnp.int32),
            V((POSES, NY), jnp.int32),
            V((8, 128, 1024), BF16), V((8, 128, 1024), BF16), V((8, 128, 1024), BF16),
            V((8, 128, 1024), BF16), V((128, 128), F32),
            V((8, CLS, 32, 128), BF16), V((NZ, 128), BF16),
            V((8, 128), F32), V((8, 128), F32), V((8, 8, 128), F32),
            V((3, RING, PLANE, THIRD, 128), BF16),
            V((8, 128), F32), V((8, 128), F32),
            V((8, K, 128), F32), V((8, NXH, 1024), BF16),
            V((8, 48, 128), BF16), V((8, 48, 128), BF16),
            V((3, RING, PLANE, THIRD, 128), BF16), V((3, RING - 1, PLANE, THIRD, 128), BF16),
            V((3, PLANE, THIRD, 128), BF16), V((3, PLANE - 1, THIRD, 128), BF16),
            V((8, CLS, 32, 128), BF16), V((8, 32, CLS * NXH), BF16), V((8, 32, CLS * NXH), BF16),
            V((K, 64), F32), V((CLS, 32, 512), BF16),
            dma((10,)), dma((3,)), dma((3,)), dma, dma, dma, dma,
            dma, dma((3, 3)), dma, dma((3,)), dma, dma, dma, dma((3, 3)), dma, dma((3,)),
            dma((2,)), dma((2,)), dma, dma,
        ],
        compiler_params=pltpu.CompilerParams(
            collective_id=0, has_side_effects=True, vmem_limit_bytes=60 * 2**20
        ),
    )(
        volume, images, defocus.reshape(1, 64), inv_noise.reshape(NY, NX2),
        class_idx.T, pose_idx.T, slab_offset,
    )
    weights, data_acc, weight_acc = pl.pallas_call(
        place,
        out_shape=tuple(jax.ShapeDtypeStruct(a.shape, a.dtype) for a in (weights, data_acc, weight_acc)),
        in_specs=[anywhere] * 3,
        out_specs=(anywhere,) * 3,
        scratch_shapes=[V(a.shape, a.dtype) for a in (weights, data_acc, weight_acc)] + [dma((2, 3))],
        compiler_params=pltpu.CompilerParams(vmem_limit_bytes=60 * 2**20),
    )(weights, data_acc, weight_acc)
    return weights.T, data_acc, weight_acc


def solution(mesh):
    return jax.shard_map(
        body,
        mesh=mesh,
        in_specs=(
            P(None, "vol", "dom"),
            P(("dom", "vol"), None),
            P(("dom", "vol")),
            P(),
            P(("dom", "vol"), None),
            P(("dom", "vol"), None),
            P(),
        ),
        out_specs=(P(("dom", "vol"), None), P(None, "vol", "dom"), P(None, "vol", "dom")),
        check_vma=False,
    )
```

```python
import functools
import math

import jax
import jax.numpy as jnp
import numpy as np
from jax import lax
from jax.experimental import pallas as pl
from jax.experimental.pallas import tpu as pltpu
from jax.sharding import PartitionSpec as P

MESH = pl.DeviceIdType.MESH
F32 = jnp.float32
BF16 = jnp.bfloat16

CLS = 4
NZ = 256
NY = 128
NXH = 64
NX2 = 128
POSES = 24
K = 4
CANDS = 96
THIRD = 32
RING = 4
PLANE = 16

PLACES = (
    (0, 0), (0, 1), (0, 3), (1, 0), (3, 0),
    (0, 2), (2, 0), (1, 1), (1, 3), (3, 1), (3, 3),
    (1, 2), (3, 2), (2, 1), (2, 3), (2, 2),
)
PLACE_OF = {step: i for i, step in enumerate(PLACES)}
BACK_OF = [PLACE_OF[(-a) % 4, (-b) % 4] for a, b in PLACES]
CLASSES = ((0, 5), (5, 11), (11, 16))
RS_CLASSES = ((0, 11), (11, 16))
CLASS_OF = [0] * 5 + [1] * 6 + [2] * 5


def around(axis, turn, place):
    first, second = PLACES[place]
    return ((turn, first, second), (first, turn, second), (first, second, turn))[axis]


def sine_coefficients(terms):
    nodes = 0.5 * np.cos((np.arange(200) + 0.5) * math.pi / 400)
    table = np.stack([nodes ** (2 * k + 1) for k in range(terms)], axis=1)
    return np.linalg.lstsq(table, np.sin(2 * math.pi * nodes), rcond=None)[0].tolist()


SINE = sine_coefficients(5)
ROUNDER = 12582912.0


def sine_of_turns(turns):
    rest = turns - ((turns + ROUNDER) - ROUNDER)
    square = rest * rest
    value = SINE[-1] * square + SINE[-2]
    for coefficient in SINE[-3::-1]:
        value = value * square + coefficient
    return value * rest


def nt_dot(left, right):
    return lax.dot_general(left, right, (((1,), (1,)), ((), ())), preferred_element_type=F32)


def dot(left, right):
    return jnp.dot(left, right, preferred_element_type=F32)


def kernel(
    volume, images, defocus, inv_noise, class_idx, pose_idx, slab_offset,
    weights_out, data_out, weight_out,
    focus_in, noise, cls_in, pose_in, slab_in,
    imgs, signal, scaled, quad, focus,
    volrow, back,
    meta_own, meta_sib, meta_all,
    sl,
    part_own, part_sib,
    w_all, ctf_sq, sq_part, sq_in,
    parts, incoming, sums, last,
    data_send, w_send, w_recv, w_held, sq_held,
    local_sem, sib_send, sib_recv, vol_send, vol_recv, meta_send, meta_recv,
    ag_send, ag_recv, ring_send, ring_recv, w_send_sem, w_recv_sem, rs_send, rs_recv, fin_send, fin_recv,
    out_send, out_recv, sq_send, sq_recv,
):
    dom = lax.axis_index("dom")
    vol = lax.axis_index("vol")
    x = (dom // 8) * 2 + vol % 2
    y = (dom // 2) % 4
    z = vol // 2
    c = dom % 2
    row = dom * 8 + vol

    def device(px, py, pz, pc):
        return ((px // 2) * 8 + py * 2 + pc, pz * 2 + px % 2)

    def near(dx, dy, dz):
        return (x + dx) % 4, (y + dy) % 4, (z + dz) % 4

    def send(src, dst, send_sem, recv_sem, target):
        pltpu.make_async_remote_copy(
            src_ref=src, dst_ref=dst, send_sem=send_sem, recv_sem=recv_sem,
            device_id=target, device_id_type=MESH,
        ).start()

    under_way = {}

    def due(ref, sem):
        name = object()
        under_way[name] = (ref, sem)

        def now():
            del under_way[name]
            pltpu.make_async_copy(ref, ref, sem).wait()

        return now

    def load(src, dst, sem):
        pltpu.make_async_copy(src, dst, sem).start()
        return due(dst, sem)

    sibling = device(x, y, z, 1 - c)

    def at(steps):
        return device(*near(*steps), c)

    barrier = pltpu.get_barrier_semaphore()
    pl.semaphore_signal(barrier, inc=1, device_id=sibling, device_id_type=MESH)
    for k in range(1, 8):
        pl.semaphore_signal(barrier, inc=1, device_id=(dom, (vol + k) % 8), device_id_type=MESH)
        pl.semaphore_signal(barrier, inc=1, device_id=((dom + 2 * k) % 16, vol), device_id_type=MESH)

    def own_images(b):
        return images.at[:, pl.ds(pl.multiple_of((2 * b + c) * 1024, 1024), 1024)]

    def other_images(b):
        return images.at[:, pl.ds(pl.multiple_of((2 * b + 1 - c) * 1024, 1024), 1024)]

    mine = pl.ds(pl.multiple_of(c * 64, 64), 64)
    own_lanes = pl.ds(pl.multiple_of(vol * 128, 128), 128)
    own_volume = load(volume.at[:, :, own_lanes], volrow.at[vol], local_sem.at[1])
    for b in range(8):
        pltpu.make_async_copy(own_images(b), imgs.at[b, mine], local_sem.at[0]).start()
    local_images = due(imgs.at[:, 0:64], local_sem.at[0])
    small = [
        load(class_idx, cls_in, local_sem.at[3]),
        load(pose_idx, pose_in, local_sem.at[4]),
        load(defocus, focus_in, local_sem.at[5]),
        load(slab_offset, slab_in, local_sem.at[6]),
        load(inv_noise, noise, local_sem.at[7]),
    ]
    pl.semaphore_wait(barrier, 15)

    vol_steps = ((2, 1), (1, 1), (3, 1), (2, 0), (1, 0), (3, 0), (0, 1))
    members = [((z + dz) % 4) * 2 + (vol + dx) % 2 for dz, dx in vol_steps]
    for pv in members:
        send(
            volume.at[:, :, pl.ds(pl.multiple_of(pv * 128, 128), 128)], volrow.at[vol],
            vol_send, vol_recv, (dom, pv),
        )
    volume_rows = due(volrow.at[0:7], vol_recv)
    due(volrow.at[0:7], vol_send)
    for b in range(8):
        send(other_images(b), imgs.at[b, mine], sib_send.at[1], sib_recv.at[1], sibling)
    for arrived in small:
        arrived()

    pair = (cls_in[...] * POSES + pose_in[...]).astype(F32)
    meta_own[...] = jnp.concatenate(
        [jnp.concatenate([pair, focus_in[...], jnp.zeros((3, 64), F32)], axis=0), jnp.zeros((8, 64), F32)], axis=1
    )

    send(meta_own, meta_sib, sib_send.at[0], sib_recv.at[0], sibling)
    sibling_meta = due(meta_sib, sib_recv.at[0])
    due(meta_own, sib_send.at[0])
    sibling_images = due(imgs.at[:, 0:64], sib_recv.at[1])
    due(imgs.at[:, 0:64], sib_send.at[1])

    sibling_meta()
    lane8 = lax.broadcasted_iota(jnp.int32, (8, 128), 1)
    first = jnp.where(c == 0, meta_own[...], meta_sib[...])
    second = jnp.where(c == 0, meta_sib[...], meta_own[...])
    meta = jnp.where(lane8 < 64, first, pltpu.roll(second, 64, 1))
    meta_all[0] = meta
    for k in range(1, 8):
        send(meta_all.at[0], meta_all.at[8 - k], meta_send, meta_recv, ((dom + 2 * k) % 16, vol))
    due(meta_all.at[0:7], meta_send)
    dom_meta = due(meta_all.at[0:7], meta_recv)
    columns = jnp.transpose(jnp.concatenate([meta, jnp.zeros((120, 128), F32)], axis=0))
    focus[...] = jnp.broadcast_to(columns[:, 4:5], (128, 128))

    lane_row = lax.broadcasted_iota(jnp.int32, (1, 128), 1) % NXH
    kx_sq = (lane_row * lane_row).astype(F32)
    turn = 6.0 / (2.0 * math.pi * (NY // 2) ** 2)

    def prepare(step, carry):
        px, py, pz = near(step // 16, (step // 4) % 4, step % 4)
        b = (px // 2) * 4 + py
        v = pz * 2 + px % 2
        r = (2 * b + c) * 8 + v
        ky = jnp.where(r < NY // 2, r, r - NY)
        squares = (kx_sq + (ky * ky).astype(F32)) * turn
        lanes = pl.ds(pl.multiple_of(v * 128, 128), 128)
        group = step // 8
        spot = pl.ds(pl.multiple_of((step % 8) * 128, 128), 128)
        contrast = -sine_of_turns(focus[...] * squares + 0.1 / (2.0 * math.pi))
        seen = contrast * imgs[b, :, lanes].astype(F32)
        level = noise[pl.ds(r, 1), :]
        signal[group, :, spot] = seen.astype(BF16)
        scaled[group, :, spot] = (seen * level).astype(BF16)
        quad[group, :, spot] = (contrast * contrast * (-0.5 * level)).astype(BF16)
        return carry

    local_images()
    sibling_images()
    lax.fori_loop(0, 4, prepare, 0)

    lane24 = lax.broadcasted_iota(jnp.int32, (POSES, 128), 1)
    offset = jnp.sum(jnp.where(lane24 == row, slab_in[...].astype(F32), 0.0), axis=1, keepdims=True)
    offset = offset.astype(jnp.int32)
    whole = lax.shift_right_arithmetic(offset, 4)
    lower = lax.bitwise_and(whole, NZ - 1)
    upper = lax.bitwise_and(whole + 1, NZ - 1)
    fraction = lax.bitwise_and(offset, 15).astype(F32) * (1.0 / 16.0)
    slab = lax.broadcasted_iota(jnp.int32, (POSES, NZ), 1)
    interp = jnp.where(slab == lower, 1.0 - fraction, 0.0) + jnp.where(slab == upper, fraction, 0.0)
    padded = jnp.concatenate([interp, interp, jnp.zeros((128 - 2 * POSES, NZ), F32)], axis=0)
    back[...] = jnp.transpose(padded).astype(BF16)

    own_volume()
    volume_rows()
    narrow = interp.astype(BF16)
    rows = [
        dot(narrow, jnp.concatenate([volrow[j, g] for j in range(8)], axis=0)) for g in range(CLS)
    ]
    slices = jnp.concatenate(rows, axis=0).astype(BF16)
    for t in range(3):
        sl[t, 0, 0] = slices[t * THIRD : (t + 1) * THIRD]
    for place in (*range(1, 5), *range(15, 4, -1)):
        for t in range(3):
            send(
                sl.at[t, 0, 0], sl.at[t, 0, BACK_OF[place]],
                ag_send, ag_recv.at[t, CLASS_OF[place]], at(around(t, 0, place)),
            )
    planes = [
        [due(sl.at[t, 0, max(low, 1) : high], ag_recv.at[t, i]) for t in range(3)]
        for i, (low, high) in enumerate(CLASSES)
    ]
    due(sl.at[:, 0, 0:15], ag_send)
    lax.fori_loop(4, 20, prepare, 0)

    for i, (low, high) in enumerate(CLASSES):
        for t in range(3):
            planes[i][t]()
            for d in (2, 1, 3):
                send(
                    sl.at[t, 0, low:high], sl.at[t, 4 - d, low:high],
                    ring_send, ring_recv.at[t], at(around(t, d, 0)),
                )
    rest = [due(sl.at[t, 1:4], ring_recv.at[t]) for t in range(3)]
    due(sl.at[:, 1:4], ring_send)
    lax.fori_loop(20, 64, prepare, 0)

    for arrived in rest:
        arrived()

    scores = jnp.zeros((CANDS, 128), F32)
    for group in range(8):
        pieces = []
        for step in range(8 * group, 8 * group + 8):
            dx, dy, dz = step // 16, (step // 4) % 4, step % 4
            pieces.append(
                jnp.concatenate(
                    [
                        sl[0, dx, PLACE_OF[dy, dz]],
                        sl[1, dy, PLACE_OF[dx, dz]],
                        sl[2, dz, PLACE_OF[dx, dy]],
                    ],
                    axis=0,
                )
            )
        band = jnp.concatenate(pieces, axis=1)
        wide_band = band.astype(F32)
        band_sq = (wide_band * wide_band).astype(BF16)
        scores = scores + nt_dot(band, scaled[group]) + nt_dot(band_sq, quad[group])
    sub96 = lax.broadcasted_iota(jnp.int32, (CANDS, 128), 0).astype(F32)
    picked = [
        jnp.sum(jnp.where(sub96 == meta[k : k + 1], scores, 0.0), axis=0, keepdims=True) for k in range(K)
    ]
    part_own[...] = jnp.concatenate(picked + [jnp.zeros((4, 128), F32)], axis=0)
    send(part_own, part_sib, sib_send.at[2], sib_recv.at[2], sibling)
    due(part_own, sib_send.at[2])
    sibling_part = due(part_sib, sib_recv.at[2])
    sibling_part()
    both = (part_own[...] + part_sib[...])[0:K]
    best = jnp.max(both, axis=0, keepdims=True)
    grown = jnp.exp(both - best)
    weights = grown / jnp.sum(grown, axis=0, keepdims=True)
    w_all[0] = weights
    for k in range(1, 8):
        send(w_all.at[0], w_all.at[8 - k], w_send_sem, w_recv_sem, ((dom + 2 * k) % 16, vol))
    due(w_all.at[0:7], w_send_sem)
    dom_w = due(w_all.at[0:7], w_recv_sem)
    w_held[...] = jnp.where(c == 0, weights, pltpu.roll(weights, 64, 1))[:, 0:64]
    load(w_held, weights_out, local_sem.at[8])

    spread = jnp.zeros((CANDS, 128), F32)
    for k in range(K):
        spread = spread + jnp.where(sub96 == meta[k : k + 1], weights[k : k + 1], 0.0)
    spread = spread.astype(BF16)

    for group in range(8):
        band = dot(spread, signal[group]).astype(BF16)
        for i in range(8):
            step = 8 * group + i
            dx, dy, dz = step // 16, (step // 4) % 4, step % 4
            piece = band[:, i * 128 : (i + 1) * 128]
            parts[0, dx, PLACE_OF[dy, dz]] = piece[0:THIRD]
            parts[1, dy, PLACE_OF[dx, dz]] = piece[THIRD : 2 * THIRD]
            parts[2, dz, PLACE_OF[dx, dy]] = piece[2 * THIRD :]
    for i in (1, 0):
        low, high = RS_CLASSES[i]
        for d in (2, 1, 3):
            for t in range(3):
                send(
                    parts.at[t, d, low:high], incoming.at[t, d - 1, low:high],
                    rs_send, rs_recv.at[t, i], at(around(t, d, 0)),
                )
    rings = [
        [due(incoming.at[t, :, low:high], rs_recv.at[t, i]) for t in range(3)]
        for i, (low, high) in enumerate(RS_CLASSES)
    ]
    due(incoming, rs_send)

    dom_meta()
    sub64 = lax.broadcasted_iota(jnp.int32, (NXH, 128), 0)

    def square_row(step, carry):
        band_row = step // 8
        k = step % 8
        r = dom * 8 + band_row
        ky = jnp.where(r < NY // 2, r, r - NY)
        squares = (sub64 * sub64 + ky * ky).astype(F32) * turn
        wave = sine_of_turns(meta_all[k, 4:5, :] * squares + 0.1 / (2.0 * math.pi))
        ctf_sq[band_row, :, pl.ds(pl.multiple_of(k * 128, 128), 128)] = (wave * wave).astype(BF16)
        return carry

    lax.fori_loop(0, 64, square_row, 0)

    dom_w()
    blocks = []
    for k in range(8):
        block = jnp.zeros((CANDS, 128), F32)
        for j in range(K):
            block = block + jnp.where(sub96 == meta_all[k, j : j + 1, :], w_all[k, j : j + 1, :], 0.0)
        blocks.append(block.astype(BF16))
    blocks = jnp.concatenate(blocks, axis=1)
    for band_row in range(8):
        part = nt_dot(blocks, ctf_sq[band_row])
        sq_part[band_row] = jnp.concatenate([part[0:48], part[48:96]], axis=1).astype(BF16)
    sq_in[vol] = sq_part[vol]
    for pv in members:
        send(sq_part.at[pv], sq_in.at[vol], sq_send, sq_recv, (dom, pv))
    due(sq_part.at[0:7], sq_send)
    vol_parts = due(sq_in.at[0:7], sq_recv)

    for i in (1, 0):
        low, high = RS_CLASSES[i]
        for t in range(3):
            rings[i][t]()
            for place in range(high - 1, low - 1, -1):
                total = parts[t, 0, place].astype(F32)
                for d in range(3):
                    total = total + incoming[t, d, place].astype(F32)
                sums[t, place] = total.astype(BF16)
                if place > 0:
                    send(
                        sums.at[t, place], last.at[t, BACK_OF[place] - 1],
                        fin_send, fin_recv.at[t], at(around(t, 0, place)),
                    )
    finals = [due(last.at[t], fin_recv.at[t]) for t in range(3)]
    due(last, fin_send)

    vol_parts()
    folded = sq_in[0].astype(F32)
    for j in range(1, 8):
        folded = folded + sq_in[j].astype(F32)
    weight_slices = jnp.concatenate([folded[:, 0:NXH], folded[:, NXH:]], axis=0)

    def backproject(classes):
        flat = jnp.concatenate(classes, axis=1)
        high = flat.astype(BF16).astype(F32)
        stacked = jnp.concatenate(
            [high, flat - high, jnp.zeros((128 - 2 * POSES, flat.shape[1]), F32)], axis=0
        )
        return dot(back[...], stacked.astype(BF16)).astype(BF16)

    result = backproject([weight_slices[g * POSES : (g + 1) * POSES] for g in range(CLS)])
    for j in range(8):
        w_send[j] = result[j * 32 : (j + 1) * 32]
    w_recv[vol] = w_send[vol]
    for pv in members:
        send(w_send.at[pv], w_recv.at[vol], out_send.at[0], out_recv.at[0], (dom, pv))
    due(w_send.at[0:7], out_send.at[0])
    weight_rows = due(w_recv.at[0:7], out_recv.at[0])

    own = []
    for g in range(CLS):
        while len(own) * THIRD < (g + 1) * POSES:
            t = len(own)
            finals[t]()
            total = sums[t, 0].astype(F32)
            for j in range(PLANE - 1):
                total = total + last[t, j].astype(F32)
            own.append(total)
        joined = jnp.concatenate(own, axis=0)
        result = backproject([joined[g * POSES : (g + 1) * POSES]])
        for j in range(8):
            data_send[j, g] = result[j * 32 : (j + 1) * 32]
        for pv in members:
            send(data_send.at[pv, g], data_out.at[g, :, own_lanes], out_send.at[1], out_recv.at[1], (dom, pv))
    due(data_send.at[0:7], out_send.at[1])
    due(data_send.at[0:7], out_recv.at[1])
    load(data_send.at[vol], data_out.at[:, :, own_lanes], local_sem.at[2])

    weight_rows()
    for pair_of in range(4):
        even = w_recv[2 * pair_of].astype(F32)
        odd = w_recv[2 * pair_of + 1].astype(F32)
        for g in range(CLS):
            lanes = slice(g * NXH, (g + 1) * NXH)
            sq_held[g, :, pair_of * 128 : (pair_of + 1) * 128] = jnp.concatenate(
                [even[:, lanes], odd[:, lanes]], axis=1
            ).astype(BF16)

    load(sq_held, weight_out, local_sem.at[9])

    for ref, sem in under_way.values():
        pltpu.make_async_copy(ref, ref, sem).wait()


def place(weights, data, squares, weights_out, data_out, weight_out, w_held, d_held, s_held, sems):
    chain = ((weights, w_held, weights_out), (data, d_held, data_out), (squares, s_held, weight_out))
    inward = [pltpu.make_async_copy(src, held, sems.at[0, i]) for i, (src, held, _) in enumerate(chain)]
    outward = [pltpu.make_async_copy(held, dst, sems.at[1, i]) for i, (_, held, dst) in enumerate(chain)]
    for copy in inward:
        copy.start()
    for first, second in zip(inward, outward):
        first.wait()
        second.start()
    for copy in outward:
        copy.wait()


def body(volume, images, defocus, inv_noise, class_idx, pose_idx, slab_offset):
    anywhere = pl.BlockSpec(memory_space=pl.ANY)
    dma = pltpu.SemaphoreType.DMA
    V = pltpu.VMEM
    weights, data_acc, weight_acc = pl.pallas_call(
        kernel,
        out_shape=(
            jax.ShapeDtypeStruct((K, 64), F32),
            jax.ShapeDtypeStruct((CLS, 32, 1024), BF16),
            jax.ShapeDtypeStruct((CLS, 32, 512), BF16),
        ),
        in_specs=[anywhere] * 7,
        out_specs=(anywhere,) * 3,
        scratch_shapes=[
            V((1, 64), F32), V((NY, NX2), F32), V((K, 64), jnp.int32), V((K, 64), jnp.int32),
            V((POSES, NY), jnp.int32),
            V((8, 128, 1024), BF16), V((8, 128, 1024), BF16), V((8, 128, 1024), BF16),
            V((8, 128, 1024), BF16), V((128, 128), F32),
            V((8, CLS, 32, 128), BF16), V((NZ, 128), BF16),
            V((8, 128), F32), V((8, 128), F32), V((8, 8, 128), F32),
            V((3, RING, PLANE, THIRD, 128), BF16),
            V((8, 128), F32), V((8, 128), F32),
            V((8, K, 128), F32), V((8, NXH, 1024), BF16),
            V((8, 48, 128), BF16), V((8, 48, 128), BF16),
            V((3, RING, PLANE, THIRD, 128), BF16), V((3, RING - 1, PLANE, THIRD, 128), BF16),
            V((3, PLANE, THIRD, 128), BF16), V((3, PLANE - 1, THIRD, 128), BF16),
            V((8, CLS, 32, 128), BF16), V((8, 32, CLS * NXH), BF16), V((8, 32, CLS * NXH), BF16),
            V((K, 64), F32), V((CLS, 32, 512), BF16),
            dma((10,)), dma((3,)), dma((3,)), dma, dma, dma, dma,
            dma, dma((3, 3)), dma, dma((3,)), dma, dma, dma, dma((3, 3)), dma, dma((3,)),
            dma((2,)), dma((2,)), dma, dma,
        ],
        compiler_params=pltpu.CompilerParams(
            collective_id=0, has_side_effects=True, vmem_limit_bytes=60 * 2**20
        ),
    )(
        volume, images, defocus.reshape(1, 64), inv_noise.reshape(NY, NX2),
        class_idx.T, pose_idx.T, slab_offset,
    )
    weights, data_acc, weight_acc = pl.pallas_call(
        place,
        out_shape=tuple(jax.ShapeDtypeStruct(a.shape, a.dtype) for a in (weights, data_acc, weight_acc)),
        in_specs=[anywhere] * 3,
        out_specs=(anywhere,) * 3,
        scratch_shapes=[V(a.shape, a.dtype) for a in (weights, data_acc, weight_acc)] + [dma((2, 3))],
        compiler_params=pltpu.CompilerParams(vmem_limit_bytes=60 * 2**20),
    )(weights, data_acc, weight_acc)
    return weights.T, data_acc, weight_acc


def solution(mesh):
    return jax.shard_map(
        body,
        mesh=mesh,
        in_specs=(
            P(None, "vol", "dom"),
            P(("dom", "vol"), None),
            P(("dom", "vol")),
            P(),
            P(("dom", "vol"), None),
            P(("dom", "vol"), None),
            P(),
        ),
        out_specs=(P(("dom", "vol"), None), P(None, "vol", "dom"), P(None, "vol", "dom")),
        check_vma=False,
    )
```
